256 devices in a mesh: chan: 16 (over z, x_lo), row: 4 (over y), col: 4 (over x_hi, core).
Axes of the slice: x: 4 (x_hi: 2, x_lo: 2; x = x_hi * 2 + x_lo), y: 4, z: 8, core: 2. Of those that a mesh axis runs over, the one named last changes fastest.
Arguments:
- voltages: bfloat16 [1024, 128, 2, 2048], P(('row', 'col'), 'chan'), may hold values from -6 to 6
- fir_taps: float32 [8, 2048], replicated, may hold values from -2 to 2
Outputs:
- visibilities: float32 [256, 2, 1024, 1024], P('chan', None, 'row', 'col')
The draws below stay inside these ranges and needn't reach their ends.
All inputs are finite; a program needn't handle non-finite values.
Results may differ from the reference program's by a relative error of at most 0.0067.
Values may be sent and summed in bfloat16 or wider, within the bound.
No kernel may reach another device: no remote copies, remote signals or barrier semaphores. Data moves between devices by JAX's collectives and lax.ppermute only.
A program may use at most 64 MiB of HBM per device.

```python
import math
import jax
import jax.numpy as jnp
from jax import lax

NIN = 1024
NCH = 2048
TAPS = 8
KEEP = 256
FRAMES = 128
N_ROW = 4
N_COL = 4


def block_levels(key, extent, split, low, largest):
    loudness = 1.0
    for position, blocks in split:
        heights = jax.random.uniform(jax.random.fold_in(jax.random.fold_in(key, 6), position), (blocks,), jnp.float32, low / len(split), largest / len(split))
        loudness = loudness * jnp.repeat(jnp.exp(heights), extent[position] // blocks).reshape((-1,) + (1,) * (len(extent) - 1 - position))
    return loudness


def gaussian(key, extent, scale, most, split=(), kind=jnp.bfloat16):
    array = jax.random.normal(key, extent, jnp.float32) * scale
    if len(split) > 0:
        array = block_levels(key, extent, split, -0.22, 0.18) * array
    return jnp.clip(array, min=-most, max=most).astype(kind)


def setup_inputs(seed: int = 0) -> dict:
    key_of = jax.random.split(jax.random.key(seed), 3)
    voltages = gaussian(key_of[0], (NIN, FRAMES, 2, NCH), 1.0, 6.0, ((0, 16), (1, 16)))
    fir_taps = gaussian(key_of[1], (TAPS, NCH), TAPS ** -0.5, 2.0, (), jnp.float32)
    return dict(voltages=voltages, fir_taps=fir_taps)


def dft_table(length, kept):
    index = jnp.arange(length, dtype=jnp.int32)
    chosen = jnp.arange(kept, dtype=jnp.int32)
    phase = (index[:, None] * chosen[None, :] % length).astype(jnp.float32) * (2.0 * math.pi / length)
    cosine = jnp.cos(phase) / math.sqrt(length)
    sine = jnp.sin(phase) / math.sqrt(length)
    upper = jnp.concatenate([cosine, -sine], axis=1)
    lower = jnp.concatenate([sine, cosine], axis=1)
    return jnp.concatenate([upper, lower], axis=0).astype(jnp.bfloat16)

def reference(voltages, fir_taps):
    block_size = NIN // (N_ROW * N_COL)
    block_count = N_ROW * N_COL
    frames = voltages.reshape(NIN, FRAMES, 2 * NCH)
    padded = jnp.pad(frames, ((0, 0), (0, TAPS - 1), (0, 0)))
    taps_both = jnp.concatenate([fir_taps, fir_taps], axis=1)
    table = dft_table(NCH, KEEP).astype(jnp.float32)

    def channelize(block):
        windowed = jnp.zeros((block_size, FRAMES, 2 * NCH), jnp.float32)
        for step in range(TAPS):
            windowed = windowed + block[:, step:step + FRAMES, :].astype(jnp.float32) * taps_both[step]
        windowed = windowed.astype(jnp.bfloat16).astype(jnp.float32)
        return jnp.einsum('itm,mk->kit', windowed, table).astype(jnp.bfloat16)
    blocks = padded.reshape(block_count, block_size, FRAMES + TAPS - 1, 2 * NCH)
    spectra = lax.map(channelize, blocks)
    spectra = jnp.transpose(spectra, (1, 0, 2, 3)).reshape(2, KEEP, NIN, FRAMES)
    by_channel = jnp.moveaxis(spectra, 1, 0)

    def correlate(single):
        values = single.astype(jnp.float32)
        flipped = jnp.stack([-values[1], values[0]])
        real_part = jnp.einsum('pit,pjt->ij', values, values)
        imag_part = jnp.einsum('pit,pjt->ij', values, flipped)
        return jnp.stack([real_part, imag_part]) / jnp.float32(FRAMES)
    return lax.map(correlate, by_channel)
```

```python
import math

import jax
import jax.numpy as jnp
import numpy as np
from jax import lax
from jax.experimental import pallas as pl
from jax.experimental.pallas import tpu as pltpu
from jax.sharding import PartitionSpec as P

import ml_dtypes

NCH = 2048
KEEP = 256
TAPS = 8
ROWS = 1024
PITCH = 1024
GROUP = 16
CHUNKS = 1
LANES = 128
MIB = 1 << 20


def dft_table():
    index = np.arange(NCH, dtype=np.int64)
    chosen = np.arange(KEEP, dtype=np.int64)
    phase = (index[:, None] * chosen[None, :] % NCH).astype(np.float32) * np.float32(
        2.0 * math.pi / NCH
    )
    cosine = np.cos(phase) / np.float32(math.sqrt(NCH))
    sine = np.sin(phase) / np.float32(math.sqrt(NCH))
    upper = np.stack([cosine, -sine], axis=1)
    lower = np.stack([sine, cosine], axis=1)
    table = np.stack([upper, lower], axis=0)
    table = table.reshape(2, NCH // LANES, LANES, 2, KEEP // 2, 2)
    table = table.transpose(3, 5, 4, 1, 0, 2)
    return np.ascontiguousarray(table.reshape(2 * KEEP, 2 * NCH)).astype(ml_dtypes.bfloat16)


def spectra_kernel(x_ref, taps_ref, table_ref, own_ref, pre_ref, fir_ref, wide_ref, acc_ref):
    group = pl.program_id(0)

    @pl.when(group == 0)
    def _():
        acc_ref[...] = jnp.zeros_like(acc_ref)
        for rho in range(GROUP):
            fir_ref[pl.ds(rho * PITCH + 512, 64), :] = jnp.zeros((64, LANES), jnp.float32)

    taps = [taps_ref[k] for k in range(TAPS)]

    def filter_input(i, carry):
        frame = [x_ref[i, t].astype(jnp.float32) for t in range(TAPS)]
        for t in range(TAPS):
            total = frame[t] * taps[0]
            for k in range(1, TAPS - t):
                total = total + frame[t + k] * taps[k]
            fir_ref[pl.ds(t * 64 + i, GROUP, stride=PITCH), :] = total
        for t in range(1, TAPS):
            total = frame[0] * taps[TAPS - t]
            for f in range(1, t):
                total = total + frame[f] * taps[TAPS - t + f]
            fir_ref[pl.ds(512 + t * 64 + i, GROUP, stride=PITCH), :] = total
        return carry

    lax.fori_loop(0, 64, filter_input, 0)

    def narrow(n, carry):
        row = pl.multiple_of(n * 128, 128)
        for rho in range(GROUP):
            wide_ref[pl.ds(row, 128), pl.ds(rho * LANES, LANES)] = fir_ref[
                pl.ds(rho * PITCH + row, 128), :
            ].astype(jnp.bfloat16)
        return carry

    lax.fori_loop(0, ROWS // 128, narrow, 0)

    def transform(n, carry):
        row = pl.multiple_of(n * 256, 256)
        acc_ref[:, pl.ds(row, 256)] += lax.dot_general(
            table_ref[...],
            wide_ref[pl.ds(row, 256), :],
            (((1,), (1,)), ((), ())),
            preferred_element_type=jnp.float32,
        )
        return carry

    lax.fori_loop(0, ROWS // 256, transform, 0)

    @pl.when(group == pl.num_programs(0) - 1)
    def _():
        low = lax.broadcasted_iota(jnp.int32, (128, LANES), 1) < 64
        for half in range(2):
            for t2 in range(4):
                lanes = pl.ds((half * 4 + t2) * LANES, LANES)
                for p in range(2):
                    zero = acc_ref[pl.ds(p * 256, 128), lanes]
                    one = acc_ref[pl.ds(p * 256 + 128, 128), lanes]
                    even = jnp.where(low, zero, pltpu.roll(one, 64, 1))
                    odd = jnp.where(low, pltpu.roll(zero, 64, 1), one)
                    row = half * 2048 + p * 8 + 2 * t2
                    fir_ref[pl.ds(row, 128, stride=16), :] = even
                    fir_ref[pl.ds(row + 1, 128, stride=16), :] = odd
        own_ref[...] = fir_ref[pl.ds(0, 2048), :]
        pre_ref[...] = fir_ref[pl.ds(2048, 2048), :].astype(jnp.bfloat16)


def spectra(voltages, fir_taps, table):
    x = voltages.reshape(64, 8, 2, 16, LANES).transpose(0, 1, 3, 2, 4).reshape(64, 8, 32, LANES)
    taps = fir_taps.reshape(TAPS, 16, 1, LANES)
    taps = jnp.broadcast_to(taps, (TAPS, 16, 2, LANES)).reshape(TAPS, 32, LANES)
    return pl.pallas_call(
        spectra_kernel,
        grid=(32 // GROUP,),
        in_specs=[
            pl.BlockSpec((64, 8, GROUP, LANES), lambda g: (0, 0, g, 0)),
            pl.BlockSpec((TAPS, GROUP, LANES), lambda g: (0, g, 0)),
            pl.BlockSpec((512, GROUP * LANES), lambda g: (0, g)),
        ],
        out_specs=[
            pl.BlockSpec((2048, LANES), lambda g: (0, 0)),
            pl.BlockSpec((2048, LANES), lambda g: (0, 0)),
        ],
        out_shape=[
            jax.ShapeDtypeStruct((2048, LANES), jnp.float32),
            jax.ShapeDtypeStruct((2048, LANES), jnp.bfloat16),
        ],
        scratch_shapes=[
            pltpu.VMEM((GROUP * PITCH, LANES), jnp.float32),
            pltpu.VMEM((ROWS, GROUP * LANES), jnp.bfloat16),
            pltpu.VMEM((512, ROWS), jnp.float32),
        ],
        compiler_params=pltpu.CompilerParams(vmem_limit_bytes=40 * MIB),
        cost_estimate=pl.CostEstimate(
            flops=2 * 1024 * 4096 * 512, bytes_accessed=12 * MIB, transcendentals=0
        ),
    )(x, taps, table)


def correlate_kernel(place_ref, *refs):
    rows, cols, out_ref, side_ref = refs[:4], refs[4:8], refs[-2], refs[-1]
    low = lax.broadcasted_iota(jnp.int32, (256, LANES), 1) < 64
    for k in range(4):
        side_ref[place_ref[k]] = rows[k][...].reshape(256, LANES).astype(jnp.float32)
        side_ref[4 + place_ref[4 + k]] = cols[k][...].reshape(256, LANES).astype(jnp.float32)

    def joined(first, channel):
        parts = []
        for b in (first, first + 2):
            left, right = side_ref[b], side_ref[b + 1]
            if channel == 0:
                parts.append(jnp.where(low, left, pltpu.roll(right, 64, 1)))
            else:
                parts.append(jnp.where(low, pltpu.roll(left, 64, 1), right))
        return jnp.concatenate(parts, axis=1)

    for channel in range(2):
        left = joined(0, channel).astype(jnp.bfloat16)
        right = joined(4, channel)
        pairs = right.reshape(16, 2, 8, 256)
        flipped = jnp.concatenate([-pairs[:, 1:], pairs[:, :1]], axis=1).reshape(256, 256)
        for part, other in ((0, right), (1, flipped)):
            out_ref[channel, part] = lax.dot_general(
                left,
                other.astype(jnp.bfloat16),
                (((0,), (0,)), ((), ())),
                preferred_element_type=jnp.float32,
            ) * (1.0 / 128.0)


def correlate(place, rows, cols, chunk, earlier):
    steps = 8 // CHUNKS
    in_specs = [pl.BlockSpec((16, 16, LANES), lambda g, place: (0, g, 0)) for _ in range(8)]
    operands = [*rows, *cols]
    aliases = {}
    if earlier is not None:
        in_specs.append(pl.BlockSpec(memory_space=pl.ANY))
        operands.append(earlier)
        aliases = {9: 0}
    return pl.pallas_call(
        correlate_kernel,
        grid_spec=pltpu.PrefetchScalarGridSpec(
            num_scalar_prefetch=1,
            grid=(steps,),
            in_specs=in_specs,
            out_specs=pl.BlockSpec(
                (2, 2, 256, 256), lambda g, place: (chunk * steps + g, 0, 0, 0)
            ),
            scratch_shapes=[pltpu.VMEM((8, 256, LANES), jnp.float32)],
        ),
        out_shape=jax.ShapeDtypeStruct((16, 2, 256, 256), jnp.float32),
        input_output_aliases=aliases,
        compiler_params=pltpu.CompilerParams(vmem_limit_bytes=24 * MIB),
        cost_estimate=pl.CostEstimate(
            flops=2**30 // CHUNKS, bytes_accessed=12 * MIB // CHUNKS, transcendentals=0
        ),
    )(place, *operands)


def per_device(voltages, fir_taps, table):
    own, pre = spectra(voltages, fir_taps, table)
    own = own.reshape(16, CHUNKS, 128 // CHUNKS, LANES)
    pre = pre.reshape(16, CHUNKS, 128 // CHUNKS, LANES)
    row, col = lax.axis_index("row"), lax.axis_index("col")
    row_places = [col ^ k for k in range(4)]
    col_places = [row, (row + 3) % 4, (row + 1) % 4, (row + 2) % 4]
    place = jnp.stack(row_places + col_places).astype(jnp.int32)
    back = [(s, s - 1) for s in range(1, 16)]
    ring = range(4)
    result = None
    for chunk in range(CHUNKS):
        rim = lax.ppermute(pre[:, chunk], "chan", back)
        whole = (own[:, chunk] + rim.astype(jnp.float32)).astype(jnp.bfloat16)
        turned = lax.all_to_all(whole, "chan", split_axis=0, concat_axis=0, tiled=True)
        crossed = lax.ppermute(
            turned, ("row", "col"), [(4 * r + c, 4 * c + r) for r in ring for c in ring]
        )
        far = lax.ppermute(turned, "col", [(c, c ^ 2) for c in ring])
        near = lax.ppermute(turned, "col", [(c, c ^ 1) for c in ring])
        both = lax.ppermute(far, "col", [(c, c ^ 1) for c in ring])
        cols = [crossed] + [
            lax.ppermute(crossed, "row", [(r, (r + d) % 4) for r in ring]) for d in (1, 3, 2)
        ]
        result = correlate(place, [turned, near, far, both], cols, chunk, result)
    return result


def solution(mesh):
    table = dft_table()

    def run(voltages, fir_taps):
        return jax.shard_map(
            per_device,
            mesh=mesh,
            in_specs=(P(("row", "col"), "chan", None, None), P(), P()),
            out_specs=P("chan", None, "row", "col"),
            check_vma=False,
        )(voltages, fir_taps, jnp.asarray(table))

    return run
```

```python
import functools
import math

import jax
import jax.numpy as jnp
import numpy as np
from jax import lax
from jax.experimental import pallas as pl
from jax.experimental.pallas import tpu as pltpu
from jax.sharding import PartitionSpec as P

import ml_dtypes

NCH = 2048
KEEP = 256
TAPS = 8
PITCH = 521
VLIM = 56
GROUP = 16
CHUNKS = 1
LANES = 128
MIB = 1 << 20


def dft_table():
    index = np.arange(NCH, dtype=np.int64)
    chosen = np.arange(KEEP, dtype=np.int64)
    phase = (index[:, None] * chosen[None, :] % NCH).astype(np.float32) * np.float32(
        2.0 * math.pi / NCH
    )
    cosine = np.cos(phase) / np.float32(math.sqrt(NCH))
    sine = np.sin(phase) / np.float32(math.sqrt(NCH))
    upper = np.stack([cosine, -sine], axis=1)
    lower = np.stack([sine, cosine], axis=1)
    table = np.stack([upper, lower], axis=0)
    table = table.reshape(2, NCH // LANES, LANES, 2, KEEP // 2, 2)
    table = table.transpose(3, 5, 4, 1, 0, 2)
    return np.ascontiguousarray(table.reshape(2 * KEEP, 2 * NCH)).astype(ml_dtypes.bfloat16)


def spectra_kernel(rim, x_ref, taps_ref, table_ref, out_ref, fir_ref, wide_ref, acc_ref):
    group = pl.program_id(0)

    @pl.when(group == 0)
    def _():
        acc_ref[...] = jnp.zeros_like(acc_ref)
        if rim:
            for rho in range(GROUP):
                fir_ref[pl.ds(rho * PITCH, 64), :] = jnp.zeros((64, LANES), jnp.float32)

    taps = [taps_ref[k] for k in range(TAPS)]

    def filter_input(i, carry):
        frame = [x_ref[i, t].astype(jnp.float32) for t in range(TAPS)]
        for t in range(1 if rim else 0, TAPS):
            pairs = [(f, TAPS - t + f) for f in range(t)] if rim else [
                (t + k, k) for k in range(TAPS - t)
            ]
            total = None
            for f, k in pairs:
                term = frame[f] * taps[k]
                total = term if total is None else total + term
            fir_ref[pl.ds(t * 64 + i, GROUP, stride=PITCH), :] = total
        return carry

    lax.fori_loop(0, 64, filter_input, 0)

    def transform(n, carry):
        row = pl.multiple_of(n * 256, 256)
        for rho in range(GROUP):
            wide_ref[:, pl.ds(rho * LANES, LANES)] = fir_ref[
                pl.ds(rho * PITCH + row, 256), :
            ].astype(jnp.bfloat16)
        acc_ref[:, pl.ds(row, 256)] += lax.dot_general(
            table_ref[...],
            wide_ref[...],
            (((1,), (1,)), ((), ())),
            preferred_element_type=jnp.float32,
        )
        return carry

    lax.fori_loop(0, 2, transform, 0)

    @pl.when(group == pl.num_programs(0) - 1)
    def _():
        low = lax.broadcasted_iota(jnp.int32, (128, LANES), 1) < 64
        for t2 in range(4):
            lanes = pl.ds(t2 * LANES, LANES)
            for p in range(2):
                zero = acc_ref[pl.ds(p * 256, 128), lanes]
                one = acc_ref[pl.ds(p * 256 + 128, 128), lanes]
                even = jnp.where(low, zero, pltpu.roll(one, 64, 1))
                odd = jnp.where(low, pltpu.roll(zero, 64, 1), one)
                row = p * 8 + 2 * t2
                fir_ref[pl.ds(row, 128, stride=17), :] = even
                fir_ref[pl.ds(row + 1, 128, stride=17), :] = odd
        for pair in range(128):
            out_ref[pl.ds(pair * 16, 16), :] = fir_ref[pl.ds(pair * 17, 16), :].astype(
                out_ref.dtype
            )


def spectra(x, taps, table, rim):
    return pl.pallas_call(
        functools.partial(spectra_kernel, rim),
        grid=(32 // GROUP,),
        in_specs=[
            pl.BlockSpec((64, 8, GROUP, LANES), lambda g: (0, 0, g, 0)),
            pl.BlockSpec((TAPS, GROUP, LANES), lambda g: (0, g, 0)),
            pl.BlockSpec((512, GROUP * LANES), lambda g: (0, g)),
        ],
        out_specs=pl.BlockSpec((2048, LANES), lambda g: (0, 0)),
        out_shape=jax.ShapeDtypeStruct((2048, LANES), jnp.bfloat16 if rim else jnp.float32),
        scratch_shapes=[
            pltpu.VMEM((GROUP * PITCH, LANES), jnp.float32),
            pltpu.VMEM((256, GROUP * LANES), jnp.bfloat16),
            pltpu.VMEM((512, 512), jnp.float32),
        ],
        compiler_params=pltpu.CompilerParams(vmem_limit_bytes=VLIM * MIB),
        cost_estimate=pl.CostEstimate(
            flops=2 * 512 * 4096 * 512, bytes_accessed=10 * MIB, transcendentals=0
        ),
    )(x, taps, table)


def prepared(voltages, fir_taps):
    x = voltages.reshape(64, 8, 2, 16, LANES).transpose(0, 1, 3, 2, 4).reshape(64, 8, 32, LANES)
    taps = fir_taps.reshape(TAPS, 16, 1, LANES)
    taps = jnp.broadcast_to(taps, (TAPS, 16, 2, LANES)).reshape(TAPS, 32, LANES)
    return x, taps


def correlate_kernel(place_ref, *refs):
    rows, cols, tails, out_ref, side_ref = refs[:4], refs[4:7], refs[7:9], refs[-2], refs[-1]
    steps = pl.num_programs(0)
    low = lax.broadcasted_iota(jnp.int32, (256, LANES), 1) < 64
    for k, block in enumerate([*rows, *cols]):
        side_ref[place_ref[k]] = block[...].reshape(256, LANES).astype(jnp.float32)
    for half, block in enumerate(tails):

        @pl.when(pl.program_id(0) // (steps // 2) == half)
        def _():
            side_ref[place_ref[7]] = block[...].reshape(256, LANES).astype(jnp.float32)

    def joined(first, channel):
        parts = []
        for b in (first, first + 2):
            left, right = side_ref[b], side_ref[b + 1]
            if channel == 0:
                parts.append(jnp.where(low, left, pltpu.roll(right, 64, 1)))
            else:
                parts.append(jnp.where(low, pltpu.roll(left, 64, 1), right))
        return jnp.concatenate(parts, axis=1)

    for channel in range(2):
        left = joined(0, channel).astype(jnp.bfloat16)
        right = joined(4, channel)
        pairs = right.reshape(16, 2, 8, 256)
        flipped = jnp.concatenate([-pairs[:, 1:], pairs[:, :1]], axis=1).reshape(256, 256)
        for part, other in ((0, right), (1, flipped)):
            out_ref[channel, part] = lax.dot_general(
                left,
                other.astype(jnp.bfloat16),
                (((0,), (0,)), ((), ())),
                preferred_element_type=jnp.float32,
            ) * (1.0 / 128.0)


def correlate(place, rows, cols, tails, chunk, earlier):
    steps = 8 // CHUNKS
    block = (16, 16, LANES)
    in_specs = [pl.BlockSpec(block, lambda g, place: (0, g, 0)) for _ in range(7)]
    in_specs.append(
        pl.BlockSpec(block, lambda g, place: (0, jnp.minimum(g, steps // 2 - 1), 0))
    )
    in_specs.append(
        pl.BlockSpec(block, lambda g, place: (0, jnp.maximum(g - steps // 2, 0), 0))
    )
    operands = [*rows, *cols, *tails]
    aliases = {}
    if earlier is not None:
        in_specs.append(pl.BlockSpec(memory_space=pl.ANY))
        operands.append(earlier)
        aliases = {10: 0}
    return pl.pallas_call(
        correlate_kernel,
        grid_spec=pltpu.PrefetchScalarGridSpec(
            num_scalar_prefetch=1,
            grid=(steps,),
            in_specs=in_specs,
            out_specs=pl.BlockSpec(
                (2, 2, 256, 256), lambda g, place: (chunk * steps + g, 0, 0, 0)
            ),
            scratch_shapes=[pltpu.VMEM((8, 256, LANES), jnp.float32)],
        ),
        out_shape=jax.ShapeDtypeStruct((16, 2, 256, 256), jnp.float32),
        input_output_aliases=aliases,
        compiler_params=pltpu.CompilerParams(vmem_limit_bytes=24 * MIB),
        cost_estimate=pl.CostEstimate(
            flops=2**30 // CHUNKS, bytes_accessed=12 * MIB // CHUNKS, transcendentals=0
        ),
    )(place, *operands)


def per_device(voltages, fir_taps, table):
    x, taps = prepared(voltages, fir_taps)
    pre = spectra(x, taps, table, True)
    own = spectra(x, taps, table, False)
    own = own.reshape(16, CHUNKS, 128 // CHUNKS, LANES)
    pre = pre.reshape(16, CHUNKS, 128 // CHUNKS, LANES)
    row, col = lax.axis_index("row"), lax.axis_index("col")
    row_places = [col ^ k for k in range(4)]
    col_places = [row, (row + 3) % 4, (row + 1) % 4, (row + 2) % 4]
    place = jnp.stack(row_places + [4 + c for c in col_places]).astype(jnp.int32)
    back = [(s, s - 1) for s in range(1, 16)]
    ring = range(4)
    result = None
    for chunk in range(CHUNKS):
        rim = lax.ppermute(pre[:, chunk], "chan", back)
        whole = (own[:, chunk] + rim.astype(jnp.float32)).astype(jnp.bfloat16)
        turned = lax.all_to_all(whole, "chan", split_axis=0, concat_axis=0, tiled=True)
        crossed = lax.ppermute(
            turned, ("row", "col"), [(4 * r + c, 4 * c + r) for r in ring for c in ring]
        )
        far = lax.ppermute(turned, "col", [(c, c ^ 2) for c in ring])
        near = lax.ppermute(turned, "col", [(c, c ^ 1) for c in ring])
        both = lax.ppermute(far, "col", [(c, c ^ 1) for c in ring])
        lower = lax.ppermute(crossed, "row", [(r, (r + 1) % 4) for r in ring])
        upper = lax.ppermute(crossed, "row", [(r, (r - 1) % 4) for r in ring])
        half = 64 // CHUNKS
        tails = [
            lax.ppermute(lower[:, :half], "row", [(r, (r + 1) % 4) for r in ring]),
            lax.ppermute(upper[:, half:], "row", [(r, (r - 1) % 4) for r in ring]),
        ]
        result = correlate(
            place, [turned, near, far, both], [crossed, lower, upper], tails, chunk, result
        )
    return result


def solution(mesh):
    table = dft_table()

    def run(voltages, fir_taps):
        return jax.shard_map(
            per_device,
            mesh=mesh,
            in_specs=(P(("row", "col"), "chan", None, None), P(), P()),
            out_specs=P("chan", None, "row", "col"),
            check_vma=False,
        )(voltages, fir_taps, jnp.asarray(table))

    return run
```

```python
import functools
import math

import jax
import jax.numpy as jnp
import numpy as np
from jax import lax
from jax.experimental import pallas as pl
from jax.experimental.pallas import tpu as pltpu
from jax.sharding import PartitionSpec as P

import ml_dtypes

NCH = 2048
KEEP = 256
TAPS = 8
PITCH = 521
VLIM = 56
INPUTS = 16
GROUP = 16
LANES = 128
MIB = 1 << 20


def dft_table():
    index = np.arange(NCH, dtype=np.int64)
    chosen = np.arange(KEEP, dtype=np.int64)
    phase = (index[:, None] * chosen[None, :] % NCH).astype(np.float32) * np.float32(
        2.0 * math.pi / NCH
    )
    cosine = np.cos(phase) / np.float32(math.sqrt(NCH))
    sine = np.sin(phase) / np.float32(math.sqrt(NCH))
    table = np.stack([cosine, sine], axis=0)[:, : NCH // 2]
    table = table.reshape(2, NCH // 2, KEEP // 2, 2).transpose(3, 0, 2, 1)
    return np.ascontiguousarray(table.reshape(2, KEEP, NCH // 2)).astype(ml_dtypes.bfloat16)


def spectra_kernel(rim, x_ref, taps_ref, table_ref, out_ref, fir_ref, wide_ref, acc_ref):
    step = pl.program_id(0)

    if rim:

        @pl.when(step == 0)
        def _():
            for rho in range(2 * GROUP):
                fir_ref[pl.ds(rho * PITCH, 64), :] = jnp.zeros((64, LANES), jnp.float32)

    def filter_input(n, carry):
        i = step * INPUTS + n
        for piece in range(2):
            rows = slice(8 * piece, 8 * piece + 8)
            halves = []
            for part in range(2):
                taps = [taps_ref[k, pl.ds(16 * part + 8 * piece, 8), :] for k in range(TAPS)]
                frame = [
                    x_ref[n, t, pl.ds(16 * part, 16), :].astype(jnp.float32)[rows]
                    for t in range(TAPS)
                ]
                totals = []
                for t in range(1 if rim else 0, TAPS):
                    pairs = [(f, TAPS - t + f) for f in range(t)] if rim else [
                        (t + k, k) for k in range(TAPS - t)
                    ]
                    total = None
                    for f, k in pairs:
                        term = frame[f] * taps[k]
                        total = term if total is None else total + term
                    totals.append(total)
                halves.append(totals)
            for t, (early, late) in enumerate(zip(*halves), 1 if rim else 0):
                base = t * 64 + i + 8 * piece * PITCH
                fir_ref[pl.ds(base, 8, stride=PITCH), :] = early + late
                fir_ref[pl.ds(base + GROUP * PITCH, 8, stride=PITCH), :] = early - late
        return carry

    lax.fori_loop(0, INPUTS, filter_input, 0)

    @pl.when(step == pl.num_programs(0) - 1)
    def _():
        def transform(low_bit, carry):
            for p in range(2):
                for cb in range(8):
                    wide_ref[:, pl.ds(cb * LANES, LANES)] = fir_ref[
                        pl.ds((low_bit * GROUP + cb * 2 + p) * PITCH, 512), :
                    ].astype(jnp.bfloat16)
                acc_ref[low_bit, p] = lax.dot_general(
                    table_ref[low_bit],
                    wide_ref[...],
                    (((1,), (1,)), ((), ())),
                    preferred_element_type=jnp.float32,
                )
            return carry

        lax.fori_loop(0, 2, transform, 0)

        low = lax.broadcasted_iota(jnp.int32, (128, LANES), 1) < 64
        for t2 in range(4):
            lanes = pl.ds(t2 * LANES, LANES)
            for p in range(2):
                pair = []
                for low_bit in range(2):
                    cosine = acc_ref[low_bit, p, pl.ds(0, 128), lanes]
                    sine = acc_ref[low_bit, 1 - p, pl.ds(128, 128), lanes]
                    pair.append(cosine + sine if p == 0 else cosine - sine)
                zero, one = pair
                even = jnp.where(low, zero, pltpu.roll(one, 64, 1))
                odd = jnp.where(low, pltpu.roll(zero, 64, 1), one)
                row = p * 8 + 2 * t2
                fir_ref[pl.ds(row, 128, stride=17), :] = even
                fir_ref[pl.ds(row + 1, 128, stride=17), :] = odd
        for pair in range(128):
            out_ref[pl.ds(pair * 16, 16), :] = fir_ref[pl.ds(pair * 17, 16), :].astype(
                out_ref.dtype
            )


def spectra(x, taps, table, rim):
    return pl.pallas_call(
        functools.partial(spectra_kernel, rim),
        grid=(64 // INPUTS,),
        in_specs=[
            pl.BlockSpec((INPUTS, 8, 32, LANES), lambda g: (g, 0, 0, 0)),
            pl.BlockSpec((TAPS, 32, LANES), lambda g: (0, 0, 0)),
            pl.BlockSpec((2, KEEP, NCH // 2), lambda g: (0, 0, 0)),
        ],
        out_specs=pl.BlockSpec((2048, LANES), lambda g: (0, 0)),
        out_shape=jax.ShapeDtypeStruct((2048, LANES), jnp.bfloat16 if rim else jnp.float32),
        scratch_shapes=[
            pltpu.VMEM((2 * GROUP * PITCH, LANES), jnp.float32),
            pltpu.VMEM((512, NCH // 2), jnp.bfloat16),
            pltpu.VMEM((2, 2, KEEP, 512), jnp.float32),
        ],
        compiler_params=pltpu.CompilerParams(vmem_limit_bytes=VLIM * MIB),
        cost_estimate=pl.CostEstimate(
            flops=2 * 512 * 2048 * 512, bytes_accessed=6 * MIB, transcendentals=0
        ),
    )(x, taps, table)


def prepared(voltages, fir_taps):
    x = voltages.reshape(64, 8, 2, 16, LANES).transpose(0, 1, 3, 2, 4).reshape(64, 8, 32, LANES)
    taps = fir_taps.reshape(TAPS, 16, 1, LANES)
    taps = jnp.broadcast_to(taps, (TAPS, 16, 2, LANES)).reshape(TAPS, 32, LANES)
    return x, taps


def correlate_kernel(late, place_ref, *refs):
    rows, cols, out_ref = refs[:4], refs[4:8], refs[-1]
    step = pl.program_id(0)
    at = pl.ds(pl.multiple_of(step * 16, 16), 16)
    odd = place_ref[5] == 1

    def block(ref):
        return ref[:, at, :].reshape(256, LANES)

    left_blocks = [block(ref) for ref in rows]
    if late:
        tail = pl.ds(pl.multiple_of(step % 4 * 16, 16), 16)
        far = jnp.where(step < 4, cols[2][:, tail, :], cols[3][:, tail, :]).reshape(256, LANES)
        right_blocks = [
            jnp.where(odd, block(cols[1]), far), jnp.where(odd, far, block(cols[0]))
        ]
    else:
        mine = block(cols[0])
        right_blocks = [
            jnp.where(odd, block(cols[1]), mine), jnp.where(odd, mine, block(cols[2]))
        ]
    for channel in range(2):
        lanes = slice(64 * channel, 64 * channel + 64)
        left = jnp.concatenate([b[:, lanes] for b in left_blocks], axis=1)
        right = jnp.concatenate([b[:, lanes] for b in right_blocks], axis=1)
        pairs = right.astype(jnp.float32).reshape(16, 2, 8, LANES)
        flipped = jnp.concatenate([-pairs[:, 1:], pairs[:, :1]], axis=1).reshape(256, LANES)
        product = lax.dot_general(
            left,
            jnp.concatenate([right, flipped.astype(jnp.bfloat16)], axis=1),
            (((0,), (0,)), ((), ())),
            preferred_element_type=jnp.float32,
        ) * (1.0 / 128.0)
        for k in range(4):
            where = pl.ds(pl.multiple_of(place_ref[k] * 64, 64), 64)
            for part in range(2):
                out_ref[channel, part, where, :] = product[
                    k * 64 : (k + 1) * 64, part * LANES : (part + 1) * LANES
                ]


def correlate(place, rows, cols, earlier):
    late = earlier is not None
    operands = [*rows, *cols]
    in_specs = [pl.BlockSpec(memory_space=pltpu.VMEM) for _ in operands]
    aliases = {}
    if late:
        in_specs.append(pl.BlockSpec(memory_space=pl.ANY))
        aliases = {1 + len(operands): 0}
        operands.append(earlier)
    return pl.pallas_call(
        functools.partial(correlate_kernel, late),
        grid_spec=pltpu.PrefetchScalarGridSpec(
            num_scalar_prefetch=1,
            grid=(8,),
            in_specs=in_specs,
            out_specs=pl.BlockSpec(
                (2, 2, 256, LANES),
                lambda g, place: (g, 0, 0, 1 - place[4] if late else place[4]),
            ),
        ),
        out_shape=jax.ShapeDtypeStruct((16, 2, 256, 256), jnp.float32),
        input_output_aliases=aliases,
        compiler_params=pltpu.CompilerParams(vmem_limit_bytes=20 * MIB),
        cost_estimate=pl.CostEstimate(
            flops=2**29, bytes_accessed=8 * MIB, transcendentals=0
        ),
    )(place, *operands)


def per_device(voltages, fir_taps, table):
    x, taps = prepared(voltages, fir_taps)
    pre = spectra(x, taps, table, True)
    own = spectra(x, taps, table, False)
    own = own.reshape(16, 128, LANES)
    pre = pre.reshape(16, 128, LANES)
    row, col = lax.axis_index("row"), lax.axis_index("col")
    place = jnp.stack([col, col ^ 1, col ^ 2, col ^ 3, row // 2, row % 2]).astype(jnp.int32)
    ring = range(4)
    up = [(r, (r + 1) % 4) for r in ring]
    down = [(r, (r - 1) % 4) for r in ring]
    rim = lax.ppermute(pre, "chan", [(s, s - 1) for s in range(1, 16)])
    whole = (own + rim.astype(jnp.float32)).astype(jnp.bfloat16)
    turned = lax.all_to_all(whole, "chan", split_axis=0, concat_axis=0, tiled=True)
    crossed = lax.ppermute(
        turned, ("row", "col"), [(4 * r + c, 4 * c + r) for r in ring for c in ring]
    )
    far = lax.ppermute(turned, "col", [(c, c ^ 2) for c in ring])
    near = lax.ppermute(turned, "col", [(c, c ^ 1) for c in ring])
    both = lax.ppermute(far, "col", [(c, c ^ 1) for c in ring])
    lower = lax.ppermute(crossed, "row", up)
    upper = lax.ppermute(crossed, "row", down)
    tails = [lax.ppermute(lower[:, :64], "row", up), lax.ppermute(upper[:, 64:], "row", down)]
    rows = [turned, near, far, both]
    result = correlate(place, rows, [crossed, lower, upper], None)
    return correlate(place, rows, [lower, upper, *tails], result)


def solution(mesh):
    table = dft_table()

    def run(voltages, fir_taps):
        return jax.shard_map(
            per_device,
            mesh=mesh,
            in_specs=(P(("row", "col"), "chan", None, None), P(), P()),
            out_specs=P("chan", None, "row", "col"),
            check_vma=False,
        )(voltages, fir_taps, jnp.asarray(table))

    return run
```

```python
import functools
import math

import jax
import jax.numpy as jnp
import numpy as np
from jax import lax
from jax.experimental import pallas as pl
from jax.experimental.pallas import tpu as pltpu
from jax.sharding import PartitionSpec as P

import ml_dtypes

NCH = 2048
KEEP = 256
TAPS = 8
PITCH = 521
VLIM = 56
INPUTS = 8
UNROLL = 2
GROUP = 16
LANES = 128
MIB = 1 << 20


def dft_table():
    index = np.arange(NCH, dtype=np.int64)
    chosen = np.arange(KEEP, dtype=np.int64)
    phase = (index[:, None] * chosen[None, :] % NCH).astype(np.float32) * np.float32(
        2.0 * math.pi / NCH
    )
    cosine = np.cos(phase) / np.float32(math.sqrt(NCH))
    sine = np.sin(phase) / np.float32(math.sqrt(NCH))
    table = np.stack([cosine, sine], axis=0)[:, : NCH // 2]
    table = table.reshape(2, NCH // 2, KEEP // 2, 2).transpose(3, 0, 2, 1)
    return np.ascontiguousarray(table.reshape(2, KEEP, NCH // 2)).astype(ml_dtypes.bfloat16)


def spectra_kernel(
    rim, x_any, raw_ref, table_any, out_ref,
    x_ref, taps_ref, loose_ref, table_ref, fir_ref, wide_ref, acc_ref, x_sem, table_sem,
):
    blocks = 64 // INPUTS
    loads = [
        pltpu.make_async_copy(
            x_any.at[pl.ds(b * INPUTS, INPUTS)], x_ref.at[pl.ds(b * INPUTS, INPUTS)], x_sem.at[b]
        )
        for b in range(blocks)
    ]
    for load in loads:
        load.start()
    table_load = pltpu.make_async_copy(table_any, table_ref, table_sem)
    table_load.start()
    for cb in range(16):
        chunk = raw_ref[:, cb * LANES : (cb + 1) * LANES]
        for p in range(2):
            loose_ref[pl.ds(cb * 2 + p, TAPS, stride=33), :] = chunk
    for k in range(TAPS):
        taps_ref[k] = loose_ref[pl.ds(k * 33, 32), :]

    if rim:
        for rho in range(2 * GROUP):
            fir_ref[pl.ds(rho * PITCH, 64), :] = jnp.zeros((64, LANES), jnp.float32)

    def filter_input(i, carry):
        for piece in range(2):
            rows = slice(8 * piece, 8 * piece + 8)
            halves = []
            for part in range(2):
                taps = [taps_ref[k, pl.ds(16 * part + 8 * piece, 8), :] for k in range(TAPS)]
                frame = [
                    x_ref[i, t, pl.ds(16 * part, 16), :].astype(jnp.float32)[rows]
                    for t in range(TAPS)
                ]
                totals = []
                for t in range(1 if rim else 0, TAPS):
                    pairs = [(f, TAPS - t + f) for f in range(t)] if rim else [
                        (t + k, k) for k in range(TAPS - t)
                    ]
                    total = None
                    for f, k in pairs:
                        term = frame[f] * taps[k]
                        total = term if total is None else total + term
                    totals.append(total)
                halves.append(totals)
            for t, (early, late) in enumerate(zip(*halves), 1 if rim else 0):
                base = t * 64 + i + 8 * piece * PITCH
                fir_ref[pl.ds(base, 8, stride=PITCH), :] = early + late
                fir_ref[pl.ds(base + GROUP * PITCH, 8, stride=PITCH), :] = early - late
        return carry

    for b, load in enumerate(loads):
        load.wait()
        lax.fori_loop(b * INPUTS, (b + 1) * INPUTS, filter_input, 0)

    table_load.wait()
    def transform(low_bit, carry):
        for p in range(2):
            for cb in range(8):
                wide_ref[:, pl.ds(cb * LANES, LANES)] = fir_ref[
                    pl.ds((low_bit * GROUP + cb * 2 + p) * PITCH, 512), :
                ].astype(jnp.bfloat16)
            acc_ref[low_bit, p] = lax.dot_general(
                table_ref[low_bit],
                wide_ref[...],
                (((1,), (1,)), ((), ())),
                preferred_element_type=jnp.float32,
            )
        return carry

    lax.fori_loop(0, 2, transform, 0, unroll=True)

    low = lax.broadcasted_iota(jnp.int32, (128, LANES), 1) < 64
    for t2 in range(4):
        lanes = pl.ds(t2 * LANES, LANES)
        for p in range(2):
            pair = []
            for low_bit in range(2):
                cosine = acc_ref[low_bit, p, pl.ds(0, 128), lanes]
                sine = acc_ref[low_bit, 1 - p, pl.ds(128, 128), lanes]
                pair.append(cosine + sine if p == 0 else cosine - sine)
            zero, one = pair
            even = jnp.where(low, zero, pltpu.roll(one, 64, 1))
            odd = jnp.where(low, pltpu.roll(zero, 64, 1), one)
            row = p * 8 + 2 * t2
            fir_ref[pl.ds(row, 128, stride=17), :] = even
            fir_ref[pl.ds(row + 1, 128, stride=17), :] = odd
    for pair in range(128):
        out_ref[pl.ds(pair * 16, 16), :] = fir_ref[pl.ds(pair * 17, 16), :].astype(
            out_ref.dtype
        )


def spectra(x, taps, table, rim):
    return pl.pallas_call(
        functools.partial(spectra_kernel, rim),
        in_specs=[
            pl.BlockSpec(memory_space=pl.ANY),
            pl.BlockSpec(memory_space=pltpu.VMEM),
            pl.BlockSpec(memory_space=pl.ANY),
        ],
        out_specs=pl.BlockSpec(memory_space=pltpu.VMEM),
        out_shape=jax.ShapeDtypeStruct((2048, LANES), jnp.bfloat16 if rim else jnp.float32),
        scratch_shapes=[
            pltpu.VMEM((64, 8, 32, LANES), jnp.bfloat16),
            pltpu.VMEM((TAPS, 32, LANES), jnp.float32),
            pltpu.VMEM((TAPS * 33, LANES), jnp.float32),
            pltpu.VMEM((2, KEEP, NCH // 2), jnp.bfloat16),
            pltpu.VMEM((2 * GROUP * PITCH, LANES), jnp.float32),
            pltpu.VMEM((512, NCH // 2), jnp.bfloat16),
            pltpu.VMEM((2, 2, KEEP, 512), jnp.float32),
            pltpu.SemaphoreType.DMA((64 // INPUTS,)),
            pltpu.SemaphoreType.DMA,
        ],
        compiler_params=pltpu.CompilerParams(vmem_limit_bytes=VLIM * MIB),
        cost_estimate=pl.CostEstimate(
            flops=2 * 512 * 2048 * 512, bytes_accessed=6 * MIB, transcendentals=0
        ),
    )(x, taps, table)


def prepared(voltages, fir_taps):
    x = voltages.reshape(64, 8, 2, 16, LANES).transpose(0, 1, 3, 2, 4).reshape(64, 8, 32, LANES)
    return x, fir_taps


def correlate_kernel(late, place_ref, *refs):
    rows, cols, out_ref, full_ref, sem = refs[:4], refs[4:8], refs[-3], refs[-2], refs[-1]
    odd = place_ref[5] == 1
    half = 1 - place_ref[4] if late else place_ref[4]
    lane = pl.multiple_of(half * LANES, LANES)

    def store(step):
        return pltpu.make_async_copy(
            full_ref.at[step],
            out_ref.at[pl.ds(2 * step, 2), :, :, pl.ds(lane, LANES)],
            sem.at[step],
        )

    def pair_of_channels(step, carry):
        at = pl.ds(pl.multiple_of(step * 16, 16), 16)

        def block(ref):
            return ref[:, at, :].reshape(256, LANES)

        left_blocks = [block(ref) for ref in rows]
        if late:
            tail = pl.ds(pl.multiple_of(step % 4 * 16, 16), 16)
            far = jnp.where(step < 4, cols[2][:, tail, :], cols[3][:, tail, :])
            far = far.reshape(256, LANES)
            right_blocks = [
                jnp.where(odd, block(cols[1]), far), jnp.where(odd, far, block(cols[0]))
            ]
        else:
            mine = block(cols[0])
            right_blocks = [
                jnp.where(odd, block(cols[1]), mine), jnp.where(odd, mine, block(cols[2]))
            ]
        for channel in range(2):
            lanes = slice(64 * channel, 64 * channel + 64)
            left = jnp.concatenate([b[:, lanes] for b in left_blocks], axis=1)
            right = jnp.concatenate([b[:, lanes] for b in right_blocks], axis=1)
            pairs = right.astype(jnp.float32).reshape(16, 2, 8, LANES)
            flipped = jnp.concatenate([-pairs[:, 1:], pairs[:, :1]], axis=1)
            flipped = flipped.reshape(256, LANES).astype(jnp.bfloat16)
            product = lax.dot_general(
                left,
                jnp.concatenate([right, flipped], axis=1),
                (((0,), (0,)), ((), ())),
                preferred_element_type=jnp.float32,
            ) * (1.0 / 128.0)
            for k in range(4):
                where = pl.ds(pl.multiple_of(place_ref[k] * 64, 64), 64)
                for part in range(2):
                    full_ref[step, channel, part, where, :] = product[
                        k * 64 : (k + 1) * 64, part * LANES : (part + 1) * LANES
                    ]
        store(step).start()
        return carry

    lax.fori_loop(0, 8, pair_of_channels, 0, unroll=UNROLL)
    for step in range(8):
        store(step).wait()


def correlate(place, rows, cols, earlier):
    late = earlier is not None
    operands = [*rows, *cols]
    in_specs = [pl.BlockSpec(memory_space=pltpu.SMEM)]
    in_specs += [pl.BlockSpec(memory_space=pltpu.VMEM) for _ in operands]
    aliases = {}
    if late:
        in_specs.append(pl.BlockSpec(memory_space=pl.ANY))
        aliases = {1 + len(operands): 0}
        operands.append(earlier)
    return pl.pallas_call(
        functools.partial(correlate_kernel, late),
        in_specs=in_specs,
        out_specs=pl.BlockSpec(memory_space=pl.ANY),
        out_shape=jax.ShapeDtypeStruct((16, 2, 256, 256), jnp.float32),
        scratch_shapes=[
            pltpu.VMEM((8, 2, 2, 256, LANES), jnp.float32),
            pltpu.SemaphoreType.DMA((8,)),
        ],
        input_output_aliases=aliases,
        compiler_params=pltpu.CompilerParams(vmem_limit_bytes=20 * MIB),
        cost_estimate=pl.CostEstimate(
            flops=2**29, bytes_accessed=8 * MIB, transcendentals=0
        ),
    )(place, *operands)


def per_device(voltages, fir_taps, table):
    x, taps = prepared(voltages, fir_taps)
    pre = spectra(x, taps, table, True)
    own = spectra(x, taps, table, False)
    own = own.reshape(16, 128, LANES)
    pre = pre.reshape(16, 128, LANES)
    row, col = lax.axis_index("row"), lax.axis_index("col")
    place = jnp.stack([col, col ^ 1, col ^ 2, col ^ 3, row // 2, row % 2]).astype(jnp.int32)
    ring = range(4)
    up = [(r, (r + 1) % 4) for r in ring]
    down = [(r, (r - 1) % 4) for r in ring]
    rim = lax.ppermute(pre, "chan", [(s, s - 1) for s in range(1, 16)])
    whole = (own + rim.astype(jnp.float32)).astype(jnp.bfloat16)
    turned = lax.all_to_all(whole, "chan", split_axis=0, concat_axis=0, tiled=True)
    crossed = lax.ppermute(
        turned, ("row", "col"), [(4 * r + c, 4 * c + r) for r in ring for c in ring]
    )
    far = lax.ppermute(turned, "col", [(c, c ^ 2) for c in ring])
    near = lax.ppermute(turned, "col", [(c, c ^ 1) for c in ring])
    both = lax.ppermute(far, "col", [(c, c ^ 1) for c in ring])
    lower = lax.ppermute(crossed, "row", up)
    upper = lax.ppermute(crossed, "row", down)
    tails = [lax.ppermute(lower[:, :64], "row", up), lax.ppermute(upper[:, 64:], "row", down)]
    rows = [turned, near, far, both]
    result = correlate(place, rows, [crossed, lower, upper], None)
    return correlate(place, rows, [lower, upper, *tails], result)


def solution(mesh):
    table = dft_table()

    def run(voltages, fir_taps):
        return jax.shard_map(
            per_device,
            mesh=mesh,
            in_specs=(P(("row", "col"), "chan", None, None), P(), P()),
            out_specs=P("chan", None, "row", "col"),
            check_vma=False,
        )(voltages, fir_taps, jnp.asarray(table))

    return run
```

```python
import functools
import math

import jax
import jax.numpy as jnp
import numpy as np
from jax import lax
from jax.experimental import pallas as pl
from jax.experimental.pallas import tpu as pltpu
from jax.sharding import PartitionSpec as P

import ml_dtypes

NCH = 2048
KEEP = 256
TAPS = 8
PITCH = 521
INPUTS = 8
UNROLL = 2
GROUP = 16
LANES = 128
MIB = 1 << 20


def dft_table():
    index = np.arange(NCH, dtype=np.int64)
    chosen = np.arange(KEEP, dtype=np.int64)
    phase = (index[:, None] * chosen[None, :] % NCH).astype(np.float32) * np.float32(
        2.0 * math.pi / NCH
    )
    cosine = np.cos(phase) / np.float32(math.sqrt(NCH))
    sine = np.sin(phase) / np.float32(math.sqrt(NCH))
    table = np.stack([cosine, sine], axis=0)[:, : NCH // 2]
    table = table.reshape(2, NCH // 2, KEEP // 2, 2).transpose(3, 0, 2, 1)
    return np.ascontiguousarray(table.reshape(2, KEEP, NCH // 2)).astype(ml_dtypes.bfloat16)


def spectra_kernel(
    rim, x_any, raw_ref, table_any, out_ref,
    x_ref, taps_ref, loose_ref, table_ref, fir_ref, wide_ref, acc_ref, x_sem, table_sem,
):
    blocks = 64 // INPUTS
    loads = [
        pltpu.make_async_copy(
            x_any.at[pl.ds(b * INPUTS, INPUTS)], x_ref.at[pl.ds(b * INPUTS, INPUTS)], x_sem.at[b]
        )
        for b in range(blocks)
    ]
    for load in loads:
        load.start()
    table_load = pltpu.make_async_copy(table_any, table_ref, table_sem)
    table_load.start()
    for cb in range(16):
        chunk = raw_ref[:, cb * LANES : (cb + 1) * LANES]
        for p in range(2):
            loose_ref[pl.ds(cb * 2 + p, TAPS, stride=33), :] = chunk
    for k in range(TAPS):
        taps_ref[k] = loose_ref[pl.ds(k * 33, 32), :]

    if rim:
        for rho in range(2 * GROUP):
            fir_ref[pl.ds(rho * PITCH, 64), :] = jnp.zeros((64, LANES), jnp.float32)

    def filter_input(i, carry):
        for piece in range(2):
            rows = slice(8 * piece, 8 * piece + 8)
            halves = []
            for part in range(2):
                taps = [taps_ref[k, pl.ds(16 * part + 8 * piece, 8), :] for k in range(TAPS)]
                frame = [
                    x_ref[i, t, pl.ds(16 * part, 16), :].astype(jnp.float32)[rows]
                    for t in range(TAPS)
                ]
                totals = []
                for t in range(1 if rim else 0, TAPS):
                    pairs = [(f, TAPS - t + f) for f in range(t)] if rim else [
                        (t + k, k) for k in range(TAPS - t)
                    ]
                    total = None
                    for f, k in pairs:
                        term = frame[f] * taps[k]
                        total = term if total is None else total + term
                    totals.append(total)
                halves.append(totals)
            for t, (early, late) in enumerate(zip(*halves), 1 if rim else 0):
                base = t * 64 + i + 8 * piece * PITCH
                fir_ref[pl.ds(base, 8, stride=PITCH), :] = early + late
                fir_ref[pl.ds(base + GROUP * PITCH, 8, stride=PITCH), :] = early - late
        return carry

    for b, load in enumerate(loads):
        load.wait()
        lax.fori_loop(b * INPUTS, (b + 1) * INPUTS, filter_input, 0)

    table_load.wait()
    def transform(low_bit, carry):
        for p in range(2):
            for cb in range(8):
                wide_ref[:, pl.ds(cb * LANES, LANES)] = fir_ref[
                    pl.ds((low_bit * GROUP + cb * 2 + p) * PITCH, 512), :
                ].astype(jnp.bfloat16)
            acc_ref[low_bit, p] = lax.dot_general(
                table_ref[low_bit],
                wide_ref[...],
                (((1,), (1,)), ((), ())),
                preferred_element_type=jnp.float32,
            )
        return carry

    lax.fori_loop(0, 2, transform, 0, unroll=True)

    low = lax.broadcasted_iota(jnp.int32, (128, LANES), 1) < 64
    for t2 in range(4):
        lanes = pl.ds(t2 * LANES, LANES)
        for p in range(2):
            pair = []
            for low_bit in range(2):
                cosine = acc_ref[low_bit, p, pl.ds(0, 128), lanes]
                sine = acc_ref[low_bit, 1 - p, pl.ds(128, 128), lanes]
                pair.append(cosine + sine if p == 0 else cosine - sine)
            zero, one = pair
            even = jnp.where(low, zero, pltpu.roll(one, 64, 1))
            odd = jnp.where(low, pltpu.roll(zero, 64, 1), one)
            row = p * 8 + 2 * t2
            fir_ref[pl.ds(row, 128, stride=17), :] = even
            fir_ref[pl.ds(row + 1, 128, stride=17), :] = odd
    for pair in range(128):
        out_ref[pl.ds(pair * 16, 16), :] = fir_ref[pl.ds(pair * 17, 16), :].astype(
            out_ref.dtype
        )


def spectra(x, taps, table, rim):
    return pl.pallas_call(
        functools.partial(spectra_kernel, rim),
        in_specs=[
            pl.BlockSpec(memory_space=pl.ANY),
            pl.BlockSpec(memory_space=pltpu.VMEM),
            pl.BlockSpec(memory_space=pl.ANY),
        ],
        out_specs=pl.BlockSpec(memory_space=pltpu.VMEM),
        out_shape=jax.ShapeDtypeStruct((2048, LANES), jnp.bfloat16 if rim else jnp.float32),
        scratch_shapes=[
            pltpu.VMEM((64, 8, 32, LANES), jnp.bfloat16),
            pltpu.VMEM((TAPS, 32, LANES), jnp.float32),
            pltpu.VMEM((TAPS * 33, LANES), jnp.float32),
            pltpu.VMEM((2, KEEP, NCH // 2), jnp.bfloat16),
            pltpu.VMEM((2 * GROUP * PITCH, LANES), jnp.float32),
            pltpu.VMEM((512, NCH // 2), jnp.bfloat16),
            pltpu.VMEM((2, 2, KEEP, 512), jnp.float32),
            pltpu.SemaphoreType.DMA((64 // INPUTS,)),
            pltpu.SemaphoreType.DMA,
        ],
        compiler_params=pltpu.CompilerParams(vmem_limit_bytes=(56 if rim else 24) * MIB),
        cost_estimate=pl.CostEstimate(
            flops=2 * 512 * 2048 * 512, bytes_accessed=6 * MIB, transcendentals=0
        ),
    )(x, taps, table)


def prepared(voltages, fir_taps):
    x = voltages.reshape(64, 8, 2, 16, LANES).transpose(0, 1, 3, 2, 4).reshape(64, 8, 32, LANES)
    return x, fir_taps


def correlate_kernel(late, place_ref, *refs):
    if late:
        rows, cols = refs[:4], refs[4:8]
        out_ref, full_ref, sem = refs[-3:]
    else:
        rows, cols = refs[:4], list(refs[4:7])
        out_ref, full_ref, sem, mine_ref, mine_sem = refs[-5:]
        load = pltpu.make_async_copy(cols[0], mine_ref, mine_sem)
        load.start()
        load.wait()
        cols[0] = mine_ref
    odd = place_ref[5] == 1
    half = 1 - place_ref[4] if late else place_ref[4]
    lane = pl.multiple_of(half * LANES, LANES)

    def store(step):
        return pltpu.make_async_copy(
            full_ref.at[step],
            out_ref.at[pl.ds(2 * step, 2), :, :, pl.ds(lane, LANES)],
            sem.at[step],
        )

    def pair_of_channels(step, carry):
        at = pl.ds(pl.multiple_of(step * 16, 16), 16)

        def block(ref):
            return ref[:, at, :].reshape(256, LANES)

        left_blocks = [block(ref) for ref in rows]
        if late:
            tail = pl.ds(pl.multiple_of(step % 4 * 16, 16), 16)
            far = jnp.where(step < 4, cols[2][:, tail, :], cols[3][:, tail, :])
            far = far.reshape(256, LANES)
            right_blocks = [
                jnp.where(odd, block(cols[1]), far), jnp.where(odd, far, block(cols[0]))
            ]
        else:
            mine = block(cols[0])
            right_blocks = [
                jnp.where(odd, block(cols[1]), mine), jnp.where(odd, mine, block(cols[2]))
            ]
        for channel in range(2):
            lanes = slice(64 * channel, 64 * channel + 64)
            left = jnp.concatenate([b[:, lanes] for b in left_blocks], axis=1)
            right = jnp.concatenate([b[:, lanes] for b in right_blocks], axis=1)
            pairs = right.astype(jnp.float32).reshape(16, 2, 8, LANES)
            flipped = jnp.concatenate([-pairs[:, 1:], pairs[:, :1]], axis=1)
            flipped = flipped.reshape(256, LANES).astype(jnp.bfloat16)
            product = lax.dot_general(
                left,
                jnp.concatenate([right, flipped], axis=1),
                (((0,), (0,)), ((), ())),
                preferred_element_type=jnp.float32,
            ) * (1.0 / 128.0)
            for k in range(4):
                where = pl.ds(pl.multiple_of(place_ref[k] * 64, 64), 64)
                for part in range(2):
                    full_ref[step, channel, part, where, :] = product[
                        k * 64 : (k + 1) * 64, part * LANES : (part + 1) * LANES
                    ]
        store(step).start()
        return carry

    lax.fori_loop(0, 8, pair_of_channels, 0, unroll=UNROLL)
    for step in range(8):
        store(step).wait()


def correlate(place, rows, cols, earlier):
    late = earlier is not None
    operands = [*rows, *cols]
    in_specs = [pl.BlockSpec(memory_space=pltpu.SMEM)]
    in_specs += [pl.BlockSpec(memory_space=pltpu.VMEM) for _ in operands]
    scratch = [
        pltpu.VMEM((8, 2, 2, 256, LANES), jnp.float32),
        pltpu.SemaphoreType.DMA((8,)),
    ]
    if not late:
        in_specs[5] = pl.BlockSpec(memory_space=pl.ANY)
        scratch += [pltpu.VMEM((16, 128, LANES), jnp.bfloat16), pltpu.SemaphoreType.DMA]
    aliases = {}
    if late:
        in_specs.append(pl.BlockSpec(memory_space=pl.ANY))
        aliases = {1 + len(operands): 0}
        operands.append(earlier)
    return pl.pallas_call(
        functools.partial(correlate_kernel, late),
        in_specs=in_specs,
        out_specs=pl.BlockSpec(memory_space=pl.ANY),
        out_shape=jax.ShapeDtypeStruct((16, 2, 256, 256), jnp.float32),
        scratch_shapes=scratch,
        input_output_aliases=aliases,
        compiler_params=pltpu.CompilerParams(vmem_limit_bytes=20 * MIB),
        cost_estimate=pl.CostEstimate(
            flops=2**29, bytes_accessed=8 * MIB, transcendentals=0
        ),
    )(place, *operands)


def per_device(voltages, fir_taps, table):
    x, taps = prepared(voltages, fir_taps)
    pre = spectra(x, taps, table, True)
    own = spectra(x, taps, table, False)
    own = own.reshape(16, 128, LANES)
    pre = pre.reshape(16, 128, LANES)
    row, col = lax.axis_index("row"), lax.axis_index("col")
    place = jnp.stack([col, col ^ 1, col ^ 2, col ^ 3, row // 2, row % 2]).astype(jnp.int32)
    ring = range(4)
    up = [(r, (r + 1) % 4) for r in ring]
    down = [(r, (r - 1) % 4) for r in ring]
    rim = lax.ppermute(pre, "chan", [(s, s - 1) for s in range(1, 16)])
    whole = (own + rim.astype(jnp.float32)).astype(jnp.bfloat16)
    turned = lax.all_to_all(whole, "chan", split_axis=0, concat_axis=0, tiled=True)
    crossed = lax.ppermute(
        turned, ("row", "col"), [(4 * r + c, 4 * c + r) for r in ring for c in ring]
    )
    far = lax.ppermute(turned, "col", [(c, c ^ 2) for c in ring])
    near = lax.ppermute(turned, "col", [(c, c ^ 1) for c in ring])
    both = lax.ppermute(far, "col", [(c, c ^ 1) for c in ring])
    lower = lax.ppermute(crossed, "row", up)
    upper = lax.ppermute(crossed, "row", down)
    tails = [lax.ppermute(lower[:, :64], "row", up), lax.ppermute(upper[:, 64:], "row", down)]
    rows = [turned, near, far, both]
    result = correlate(place, rows, [crossed, lower, upper], None)
    return correlate(place, rows, [lower, upper, *tails], result)


def solution(mesh):
    table = dft_table()

    def run(voltages, fir_taps):
        return jax.shard_map(
            per_device,
            mesh=mesh,
            in_specs=(P(("row", "col"), "chan", None, None), P(), P()),
            out_specs=P("chan", None, "row", "col"),
            check_vma=False,
        )(voltages, fir_taps, jnp.asarray(table))

    return run
```

```python
import functools
import math

import jax
import jax.numpy as jnp
import numpy as np
from jax import lax
from jax.experimental import pallas as pl
from jax.experimental.pallas import tpu as pltpu
from jax.sharding import PartitionSpec as P

import ml_dtypes

NCH = 2048
KEEP = 256
TAPS = 8
PITCH = 521
INPUTS = 8
UNROLL = 2
GROUP = 16
LANES = 128
MIB = 1 << 20


def dft_table():
    index = np.arange(NCH, dtype=np.int64)
    chosen = np.arange(KEEP, dtype=np.int64)
    phase = (index[:, None] * chosen[None, :] % NCH).astype(np.float32) * np.float32(
        2.0 * math.pi / NCH
    )
    cosine = np.cos(phase) / np.float32(math.sqrt(NCH))
    sine = np.sin(phase) / np.float32(math.sqrt(NCH))
    table = np.stack([cosine, sine], axis=0)[:, : NCH // 2]
    table = table.reshape(2, NCH // 2, KEEP // 2, 2).transpose(3, 0, 2, 1)
    return np.ascontiguousarray(table.reshape(2, KEEP, NCH // 2)).astype(ml_dtypes.bfloat16)


def spectra_kernel(
    rim, x_any, raw_ref, table_any, out_ref,
    x_ref, taps_ref, loose_ref, table_ref, fir_ref, wide_ref, acc_ref, x_sem, table_sem,
):
    blocks = 64 // INPUTS
    loads = [
        pltpu.make_async_copy(
            x_any.at[pl.ds(b * INPUTS, INPUTS)], x_ref.at[pl.ds(b * INPUTS, INPUTS)], x_sem.at[b]
        )
        for b in range(blocks)
    ]
    for load in loads:
        load.start()
    table_load = pltpu.make_async_copy(table_any, table_ref, table_sem)
    table_load.start()
    for cb in range(16):
        chunk = raw_ref[:, cb * LANES : (cb + 1) * LANES]
        for p in range(2):
            loose_ref[pl.ds(cb * 2 + p, TAPS, stride=33), :] = chunk
    for k in range(TAPS):
        taps_ref[k] = loose_ref[pl.ds(k * 33, 32), :]

    if rim:
        for rho in range(2 * GROUP):
            fir_ref[pl.ds(rho * PITCH, 64), :] = jnp.zeros((64, LANES), jnp.float32)

    def filter_input(i, carry):
        for piece in range(2):
            rows = slice(8 * piece, 8 * piece + 8)
            halves = []
            for part in range(2):
                taps = [taps_ref[k, pl.ds(16 * part + 8 * piece, 8), :] for k in range(TAPS)]
                frame = [
                    x_ref[i, t, pl.ds(16 * part, 16), :].astype(jnp.float32)[rows]
                    for t in range(TAPS)
                ]
                totals = []
                for t in range(1 if rim else 0, TAPS):
                    pairs = [(f, TAPS - t + f) for f in range(t)] if rim else [
                        (t + k, k) for k in range(TAPS - t)
                    ]
                    total = None
                    for f, k in pairs:
                        term = frame[f] * taps[k]
                        total = term if total is None else total + term
                    totals.append(total)
                halves.append(totals)
            for t, (early, late) in enumerate(zip(*halves), 1 if rim else 0):
                base = t * 64 + i + 8 * piece * PITCH
                fir_ref[pl.ds(base, 8, stride=PITCH), :] = early + late
                fir_ref[pl.ds(base + GROUP * PITCH, 8, stride=PITCH), :] = early - late
        return carry

    for b, load in enumerate(loads):
        load.wait()
        lax.fori_loop(b * INPUTS, (b + 1) * INPUTS, filter_input, 0, unroll=4)

    table_load.wait()
    def transform(low_bit, carry):
        for p in range(2):
            for cb in range(8):
                wide_ref[:, pl.ds(cb * LANES, LANES)] = fir_ref[
                    pl.ds((low_bit * GROUP + cb * 2 + p) * PITCH, 512), :
                ].astype(jnp.bfloat16)
            acc_ref[low_bit, p] = lax.dot_general(
                table_ref[low_bit],
                wide_ref[...],
                (((1,), (1,)), ((), ())),
                preferred_element_type=jnp.float32,
            )
        return carry

    lax.fori_loop(0, 2, transform, 0, unroll=True)

    low = lax.broadcasted_iota(jnp.int32, (128, LANES), 1) < 64
    for t2 in range(4):
        lanes = pl.ds(t2 * LANES, LANES)
        for p in range(2):
            pair = []
            for low_bit in range(2):
                cosine = acc_ref[low_bit, p, pl.ds(0, 128), lanes]
                sine = acc_ref[low_bit, 1 - p, pl.ds(128, 128), lanes]
                pair.append(cosine + sine if p == 0 else cosine - sine)
            zero, one = pair
            even = jnp.where(low, zero, pltpu.roll(one, 64, 1))
            odd = jnp.where(low, pltpu.roll(zero, 64, 1), one)
            row = p * 8 + 2 * t2
            fir_ref[pl.ds(row, 128, stride=17), :] = even
            fir_ref[pl.ds(row + 1, 128, stride=17), :] = odd
    for pair in range(128):
        out_ref[pl.ds(pair * 16, 16), :] = fir_ref[pl.ds(pair * 17, 16), :].astype(
            out_ref.dtype
        )


def spectra(x, taps, table, rim):
    return pl.pallas_call(
        functools.partial(spectra_kernel, rim),
        in_specs=[
            pl.BlockSpec(memory_space=pl.ANY),
            pl.BlockSpec(memory_space=pltpu.VMEM),
            pl.BlockSpec(memory_space=pl.ANY),
        ],
        out_specs=pl.BlockSpec(memory_space=pltpu.VMEM),
        out_shape=jax.ShapeDtypeStruct((2048, LANES), jnp.bfloat16 if rim else jnp.float32),
        scratch_shapes=[
            pltpu.VMEM((64, 8, 32, LANES), jnp.bfloat16),
            pltpu.VMEM((TAPS, 32, LANES), jnp.float32),
            pltpu.VMEM((TAPS * 33, LANES), jnp.float32),
            pltpu.VMEM((2, KEEP, NCH // 2), jnp.bfloat16),
            pltpu.VMEM((2 * GROUP * PITCH, LANES), jnp.float32),
            pltpu.VMEM((512, NCH // 2), jnp.bfloat16),
            pltpu.VMEM((2, 2, KEEP, 512), jnp.float32),
            pltpu.SemaphoreType.DMA((64 // INPUTS,)),
            pltpu.SemaphoreType.DMA,
        ],
        compiler_params=pltpu.CompilerParams(vmem_limit_bytes=(56 if rim else 24) * MIB),
        cost_estimate=pl.CostEstimate(
            flops=2 * 512 * 2048 * 512, bytes_accessed=6 * MIB, transcendentals=0
        ),
    )(x, taps, table)


def prepared(voltages, fir_taps):
    x = voltages.reshape(64, 8, 2, 16, LANES).transpose(0, 1, 3, 2, 4).reshape(64, 8, 32, LANES)
    return x, fir_taps


def correlate_kernel(late, place_ref, *refs):
    if late:
        left_ref, cols = refs[0], refs[1:5]
        out_ref, full_ref, sem = refs[-3:]
    else:
        rows, cols = refs[:4], list(refs[4:7])
        out_ref, left_ref, full_ref, sem, mine_ref, mine_sem = refs[-6:]
        load = pltpu.make_async_copy(cols[0], mine_ref, mine_sem)
        load.start()
        load.wait()
        cols[0] = mine_ref
    odd = place_ref[5] == 1
    half = 1 - place_ref[4] if late else place_ref[4]
    lane = pl.multiple_of(half * LANES, LANES)

    def store(step):
        return pltpu.make_async_copy(
            full_ref.at[step],
            out_ref.at[pl.ds(2 * step, 2), :, :, pl.ds(lane, LANES)],
            sem.at[step],
        )

    def pair_of_channels(step, carry):
        at = pl.ds(pl.multiple_of(step * 16, 16), 16)

        def block(ref):
            return ref[:, at, :].reshape(256, LANES)

        if late:
            tail = pl.ds(pl.multiple_of(step % 4 * 16, 16), 16)
            far = jnp.where(step < 4, cols[2][:, tail, :], cols[3][:, tail, :])
            far = far.reshape(256, LANES)
            right_blocks = [
                jnp.where(odd, block(cols[1]), far), jnp.where(odd, far, block(cols[0]))
            ]
        else:
            left_blocks = [block(ref) for ref in rows]
            mine = block(cols[0])
            right_blocks = [
                jnp.where(odd, block(cols[1]), mine), jnp.where(odd, mine, block(cols[2]))
            ]
        for channel in range(2):
            lanes = slice(64 * channel, 64 * channel + 64)
            if late:
                left = left_ref[2 * step + channel]
            else:
                left = jnp.concatenate([b[:, lanes] for b in left_blocks], axis=1).T
                left_ref[2 * step + channel] = left
            right = jnp.concatenate([b[:, lanes] for b in right_blocks], axis=1)
            pairs = right.astype(jnp.float32).reshape(16, 2, 8, LANES)
            flipped = jnp.concatenate([-pairs[:, 1:], pairs[:, :1]], axis=1)
            flipped = flipped.reshape(256, LANES).astype(jnp.bfloat16)
            product = lax.dot_general(
                left,
                jnp.concatenate([right, flipped], axis=1),
                (((1,), (0,)), ((), ())),
                preferred_element_type=jnp.float32,
            ) * (1.0 / 128.0)
            for k in range(4):
                where = pl.ds(pl.multiple_of(place_ref[k] * 64, 64), 64)
                for part in range(2):
                    full_ref[step, channel, part, where, :] = product[
                        k * 64 : (k + 1) * 64, part * LANES : (part + 1) * LANES
                    ]
        store(step).start()
        return carry

    lax.fori_loop(0, 8, pair_of_channels, 0, unroll=UNROLL)
    for step in range(8):
        store(step).wait()


def correlate(place, rows, cols, earlier):
    late = earlier is not None
    operands = [*rows, *cols]
    in_specs = [pl.BlockSpec(memory_space=pltpu.SMEM)]
    in_specs += [pl.BlockSpec(memory_space=pltpu.VMEM) for _ in operands]
    scratch = [
        pltpu.VMEM((8, 2, 2, 256, LANES), jnp.float32),
        pltpu.SemaphoreType.DMA((8,)),
    ]
    if not late:
        in_specs[5] = pl.BlockSpec(memory_space=pl.ANY)
        scratch += [pltpu.VMEM((16, 128, LANES), jnp.bfloat16), pltpu.SemaphoreType.DMA]
    aliases = {}
    out_specs = [pl.BlockSpec(memory_space=pl.ANY)]
    out_shape = [jax.ShapeDtypeStruct((16, 2, 256, 256), jnp.float32)]
    if not late:
        out_specs.append(pl.BlockSpec(memory_space=pltpu.VMEM))
        out_shape.append(jax.ShapeDtypeStruct((16, 256, 256), jnp.bfloat16))
    if late:
        in_specs.append(pl.BlockSpec(memory_space=pl.ANY))
        aliases = {1 + len(operands): 0}
        operands.append(earlier)
    return pl.pallas_call(
        functools.partial(correlate_kernel, late),
        in_specs=in_specs,
        out_specs=out_specs,
        out_shape=out_shape,
        scratch_shapes=scratch,
        input_output_aliases=aliases,
        compiler_params=pltpu.CompilerParams(vmem_limit_bytes=20 * MIB),
        cost_estimate=pl.CostEstimate(
            flops=2**29, bytes_accessed=8 * MIB, transcendentals=0
        ),
    )(place, *operands)


def per_device(voltages, fir_taps, table):
    x, taps = prepared(voltages, fir_taps)
    pre = spectra(x, taps, table, True)
    own = spectra(x, taps, table, False)
    own = own.reshape(16, 128, LANES)
    pre = pre.reshape(16, 128, LANES)
    row, col = lax.axis_index("row"), lax.axis_index("col")
    place = jnp.stack([col, col ^ 1, col ^ 2, col ^ 3, row // 2, row % 2]).astype(jnp.int32)
    ring = range(4)
    up = [(r, (r + 1) % 4) for r in ring]
    down = [(r, (r - 1) % 4) for r in ring]
    rim = lax.ppermute(pre, "chan", [(s, s - 1) for s in range(1, 16)])
    whole = (own + rim.astype(jnp.float32)).astype(jnp.bfloat16)
    turned = lax.all_to_all(whole, "chan", split_axis=0, concat_axis=0, tiled=True)
    crossed = lax.ppermute(
        turned, ("row", "col"), [(4 * r + c, 4 * c + r) for r in ring for c in ring]
    )
    far = lax.ppermute(turned, "col", [(c, c ^ 2) for c in ring])
    near = lax.ppermute(turned, "col", [(c, c ^ 1) for c in ring])
    both = lax.ppermute(far, "col", [(c, c ^ 1) for c in ring])
    lower = lax.ppermute(crossed, "row", up)
    upper = lax.ppermute(crossed, "row", down)
    tails = [lax.ppermute(lower[:, :64], "row", up), lax.ppermute(upper[:, 64:], "row", down)]
    rows = [turned, near, far, both]
    result, left = correlate(place, rows, [crossed, lower, upper], None)
    return correlate(place, [left], [lower, upper, *tails], result)[0]


def solution(mesh):
    table = dft_table()

    def run(voltages, fir_taps):
        return jax.shard_map(
            per_device,
            mesh=mesh,
            in_specs=(P(("row", "col"), "chan", None, None), P(), P()),
            out_specs=P("chan", None, "row", "col"),
            check_vma=False,
        )(voltages, fir_taps, jnp.asarray(table))

    return run
```

```python
import functools
import math

import jax
import jax.numpy as jnp
import numpy as np
from jax import lax
from jax.experimental import pallas as pl
from jax.experimental.pallas import tpu as pltpu
from jax.sharding import PartitionSpec as P

import ml_dtypes

NCH = 2048
KEEP = 256
TAPS = 8
PITCH = 521
INPUTS = 8
UNROLL = 4
GROUP = 16
LANES = 128
MIB = 1 << 20


def dft_table():
    index = np.arange(NCH, dtype=np.int64)
    chosen = np.arange(KEEP, dtype=np.int64)
    phase = (index[:, None] * chosen[None, :] % NCH).astype(np.float32) * np.float32(
        2.0 * math.pi / NCH
    )
    cosine = np.cos(phase) / np.float32(math.sqrt(NCH))
    sine = np.sin(phase) / np.float32(math.sqrt(NCH))
    table = np.stack([cosine, sine], axis=0)[:, : NCH // 2]
    table = table.reshape(2, NCH // 2, KEEP // 2, 2).transpose(3, 0, 2, 1)
    return np.ascontiguousarray(table.reshape(2, KEEP, NCH // 2)).astype(ml_dtypes.bfloat16)


def spectra_kernel(
    rim, x_any, raw_ref, table_any, out_ref,
    x_ref, taps_ref, loose_ref, table_ref, fir_ref, wide_ref, acc_ref, x_sem, table_sem,
):
    blocks = 64 // INPUTS
    loads = [
        pltpu.make_async_copy(
            x_any.at[pl.ds(b * INPUTS, INPUTS)], x_ref.at[pl.ds(b * INPUTS, INPUTS)], x_sem.at[b]
        )
        for b in range(blocks)
    ]
    for load in loads:
        load.start()
    table_load = pltpu.make_async_copy(table_any, table_ref, table_sem)
    table_load.start()
    for cb in range(16):
        chunk = raw_ref[:, cb * LANES : (cb + 1) * LANES]
        for p in range(2):
            loose_ref[pl.ds(cb * 2 + p, TAPS, stride=33), :] = chunk
    for k in range(TAPS):
        taps_ref[k] = loose_ref[pl.ds(k * 33, 32), :]

    if rim:
        for rho in range(2 * GROUP):
            fir_ref[pl.ds(rho * PITCH, 64), :] = jnp.zeros((64, LANES), jnp.float32)

    def filter_input(i, carry):
        for piece in range(2):
            rows = slice(8 * piece, 8 * piece + 8)
            halves = []
            for part in range(2):
                taps = [taps_ref[k, pl.ds(16 * part + 8 * piece, 8), :] for k in range(TAPS)]
                frame = [
                    x_ref[i, t, pl.ds(16 * part, 16), :].astype(jnp.float32)[rows]
                    for t in range(TAPS)
                ]
                totals = []
                for t in range(1 if rim else 0, TAPS):
                    pairs = [(f, TAPS - t + f) for f in range(t)] if rim else [
                        (t + k, k) for k in range(TAPS - t)
                    ]
                    total = None
                    for f, k in pairs:
                        term = frame[f] * taps[k]
                        total = term if total is None else total + term
                    totals.append(total)
                halves.append(totals)
            for t, (early, late) in enumerate(zip(*halves), 1 if rim else 0):
                base = t * 64 + i + 8 * piece * PITCH
                fir_ref[pl.ds(base, 8, stride=PITCH), :] = early + late
                fir_ref[pl.ds(base + GROUP * PITCH, 8, stride=PITCH), :] = early - late
        return carry

    for b, load in enumerate(loads):
        load.wait()
        lax.fori_loop(b * INPUTS, (b + 1) * INPUTS, filter_input, 0, unroll=4)

    table_load.wait()
    def transform(low_bit, carry):
        for p in range(2):
            for cb in range(8):
                wide_ref[:, pl.ds(cb * LANES, LANES)] = fir_ref[
                    pl.ds((low_bit * GROUP + cb * 2 + p) * PITCH, 512), :
                ].astype(jnp.bfloat16)
            acc_ref[low_bit, p] = lax.dot_general(
                table_ref[low_bit],
                wide_ref[...],
                (((1,), (1,)), ((), ())),
                preferred_element_type=jnp.float32,
            )
        return carry

    lax.fori_loop(0, 2, transform, 0, unroll=True)

    low = lax.broadcasted_iota(jnp.int32, (128, LANES), 1) < 64
    for t2 in range(4):
        lanes = pl.ds(t2 * LANES, LANES)
        for p in range(2):
            pair = []
            for low_bit in range(2):
                cosine = acc_ref[low_bit, p, pl.ds(0, 128), lanes]
                sine = acc_ref[low_bit, 1 - p, pl.ds(128, 128), lanes]
                pair.append(cosine + sine if p == 0 else cosine - sine)
            zero, one = pair
            even = jnp.where(low, zero, pltpu.roll(one, 64, 1))
            odd = jnp.where(low, pltpu.roll(zero, 64, 1), one)
            row = p * 8 + 2 * t2
            fir_ref[pl.ds(row, 128, stride=17), :] = even
            fir_ref[pl.ds(row + 1, 128, stride=17), :] = odd
    for pair in range(128):
        out_ref[pl.ds(pair * 16, 16), :] = fir_ref[pl.ds(pair * 17, 16), :].astype(
            out_ref.dtype
        )


def spectra(x, taps, table, rim):
    return pl.pallas_call(
        functools.partial(spectra_kernel, rim),
        in_specs=[
            pl.BlockSpec(memory_space=pl.ANY),
            pl.BlockSpec(memory_space=pltpu.VMEM),
            pl.BlockSpec(memory_space=pl.ANY),
        ],
        out_specs=pl.BlockSpec(memory_space=pltpu.VMEM),
        out_shape=jax.ShapeDtypeStruct((2048, LANES), jnp.bfloat16 if rim else jnp.float32),
        scratch_shapes=[
            pltpu.VMEM((64, 8, 32, LANES), jnp.bfloat16),
            pltpu.VMEM((TAPS, 32, LANES), jnp.float32),
            pltpu.VMEM(((TAPS + 1) * 33, LANES), jnp.float32),
            pltpu.VMEM((2, KEEP, NCH // 2), jnp.bfloat16),
            pltpu.VMEM(((2 * GROUP + 1) * PITCH, LANES), jnp.float32),
            pltpu.VMEM((512, NCH // 2), jnp.bfloat16),
            pltpu.VMEM((2, 2, KEEP, 512), jnp.float32),
            pltpu.SemaphoreType.DMA((64 // INPUTS,)),
            pltpu.SemaphoreType.DMA,
        ],
        compiler_params=pltpu.CompilerParams(vmem_limit_bytes=(56 if rim else 24) * MIB),
        cost_estimate=pl.CostEstimate(
            flops=2 * 512 * 2048 * 512, bytes_accessed=6 * MIB, transcendentals=0
        ),
    )(x, taps, table)


def prepared(voltages, fir_taps):
    x = voltages.reshape(64, 8, 2, 16, LANES).transpose(0, 1, 3, 2, 4).reshape(64, 8, 32, LANES)
    return x, fir_taps


def correlate_kernel(late, place_ref, *refs):
    if late:
        left_ref, cols = refs[0], refs[1:5]
        out_ref, full_ref, sem = refs[-3:]
    else:
        rows, cols = refs[:4], list(refs[4:7])
        out_ref, left_ref, full_ref, sem, mine_ref, mine_sem = refs[-6:]
        load = pltpu.make_async_copy(cols[0], mine_ref, mine_sem)
        load.start()
        load.wait()
        cols[0] = mine_ref
    odd = place_ref[5] == 1
    half = 1 - place_ref[4] if late else place_ref[4]
    lane = pl.multiple_of(half * LANES, LANES)

    def store(step):
        return pltpu.make_async_copy(
            full_ref.at[step],
            out_ref.at[pl.ds(2 * step, 2), :, :, pl.ds(lane, LANES)],
            sem.at[step],
        )

    def pair_of_channels(step, carry):
        at = pl.ds(pl.multiple_of(step * 16, 16), 16)

        def block(ref):
            return ref[:, at, :].reshape(256, LANES)

        if late:
            tail = pl.ds(pl.multiple_of(step % 4 * 16, 16), 16)
            far = jnp.where(step < 4, cols[2][:, tail, :], cols[3][:, tail, :])
            far = far.reshape(256, LANES)
            right_blocks = [
                jnp.where(odd, block(cols[1]), far), jnp.where(odd, far, block(cols[0]))
            ]
        else:
            left_blocks = [block(ref) for ref in rows]
            mine = block(cols[0])
            right_blocks = [
                jnp.where(odd, block(cols[1]), mine), jnp.where(odd, mine, block(cols[2]))
            ]
        for channel in range(2):
            lanes = slice(64 * channel, 64 * channel + 64)
            if late:
                left = left_ref[2 * step + channel]
            else:
                left = jnp.concatenate([b[:, lanes] for b in left_blocks], axis=1).T
                left_ref[2 * step + channel] = left
            right = jnp.concatenate([b[:, lanes] for b in right_blocks], axis=1)
            pairs = right.astype(jnp.float32).reshape(16, 2, 8, LANES)
            flipped = jnp.concatenate([-pairs[:, 1:], pairs[:, :1]], axis=1)
            flipped = flipped.reshape(256, LANES).astype(jnp.bfloat16)
            product = lax.dot_general(
                left,
                jnp.concatenate([right, flipped], axis=1),
                (((1,), (0,)), ((), ())),
                preferred_element_type=jnp.float32,
            ) * (1.0 / 128.0)
            for k in range(4):
                where = pl.ds(pl.multiple_of(place_ref[k] * 64, 64), 64)
                for part in range(2):
                    full_ref[step, channel, part, where, :] = product[
                        k * 64 : (k + 1) * 64, part * LANES : (part + 1) * LANES
                    ]
        store(step).start()
        return carry

    lax.fori_loop(0, 8, pair_of_channels, 0, unroll=UNROLL)
    for step in range(8):
        store(step).wait()


def correlate(place, rows, cols, earlier):
    late = earlier is not None
    operands = [*rows, *cols]
    in_specs = [pl.BlockSpec(memory_space=pltpu.SMEM)]
    in_specs += [pl.BlockSpec(memory_space=pltpu.VMEM) for _ in operands]
    scratch = [
        pltpu.VMEM((8, 2, 2, 256, LANES), jnp.float32),
        pltpu.SemaphoreType.DMA((8,)),
    ]
    if not late:
        in_specs[5] = pl.BlockSpec(memory_space=pl.ANY)
        scratch += [pltpu.VMEM((16, 128, LANES), jnp.bfloat16), pltpu.SemaphoreType.DMA]
    aliases = {}
    out_specs = [pl.BlockSpec(memory_space=pl.ANY)]
    out_shape = [jax.ShapeDtypeStruct((16, 2, 256, 256), jnp.float32)]
    if not late:
        out_specs.append(pl.BlockSpec(memory_space=pltpu.VMEM))
        out_shape.append(jax.ShapeDtypeStruct((16, 256, 256), jnp.bfloat16))
    if late:
        in_specs.append(pl.BlockSpec(memory_space=pl.ANY))
        aliases = {1 + len(operands): 0}
        operands.append(earlier)
    return pl.pallas_call(
        functools.partial(correlate_kernel, late),
        in_specs=in_specs,
        out_specs=out_specs,
        out_shape=out_shape,
        scratch_shapes=scratch,
        input_output_aliases=aliases,
        compiler_params=pltpu.CompilerParams(vmem_limit_bytes=20 * MIB),
        cost_estimate=pl.CostEstimate(
            flops=2**29, bytes_accessed=8 * MIB, transcendentals=0
        ),
    )(place, *operands)


def per_device(voltages, fir_taps, table):
    x, taps = prepared(voltages, fir_taps)
    pre = spectra(x, taps, table, True)
    own = spectra(x, taps, table, False)
    own = own.reshape(16, 128, LANES)
    pre = pre.reshape(16, 128, LANES)
    row, col = lax.axis_index("row"), lax.axis_index("col")
    place = jnp.stack([col, col ^ 1, col ^ 2, col ^ 3, row // 2, row % 2]).astype(jnp.int32)
    ring = range(4)
    up = [(r, (r + 1) % 4) for r in ring]
    down = [(r, (r - 1) % 4) for r in ring]
    rim = lax.ppermute(pre, "chan", [(s, s - 1) for s in range(1, 16)])
    whole = (own + rim.astype(jnp.float32)).astype(jnp.bfloat16)
    turned = lax.all_to_all(whole, "chan", split_axis=0, concat_axis=0, tiled=True)
    crossed = lax.ppermute(
        turned, ("row", "col"), [(4 * r + c, 4 * c + r) for r in ring for c in ring]
    )
    far = lax.ppermute(turned, "col", [(c, c ^ 2) for c in ring])
    near = lax.ppermute(turned, "col", [(c, c ^ 1) for c in ring])
    both = lax.ppermute(far, "col", [(c, c ^ 1) for c in ring])
    lower = lax.ppermute(crossed, "row", up)
    upper = lax.ppermute(crossed, "row", down)
    tails = [lax.ppermute(lower[:, :64], "row", up), lax.ppermute(upper[:, 64:], "row", down)]
    rows = [turned, near, far, both]
    result, left = correlate(place, rows, [crossed, lower, upper], None)
    return correlate(place, [left], [lower, upper, *tails], result)[0]


def solution(mesh):
    table = dft_table()

    def run(voltages, fir_taps):
        return jax.shard_map(
            per_device,
            mesh=mesh,
            in_specs=(P(("row", "col"), "chan", None, None), P(), P()),
            out_specs=P("chan", None, "row", "col"),
            check_vma=False,
        )(voltages, fir_taps, jnp.asarray(table))

    return run
```

```python
import functools
import math

import jax
import jax.numpy as jnp
import numpy as np
from jax import lax
from jax.experimental import pallas as pl
from jax.experimental.pallas import tpu as pltpu
from jax.sharding import PartitionSpec as P

import ml_dtypes

NCH = 2048
KEEP = 256
TAPS = 8
PITCH = 521
INPUTS = 8
UNROLL = 4
GROUP = 16
LANES = 128
MIB = 1 << 20


def dft_table():
    index = np.arange(NCH, dtype=np.int64)
    chosen = np.arange(KEEP, dtype=np.int64)
    phase = (index[:, None] * chosen[None, :] % NCH).astype(np.float32) * np.float32(
        2.0 * math.pi / NCH
    )
    cosine = np.cos(phase) / np.float32(math.sqrt(NCH))
    sine = np.sin(phase) / np.float32(math.sqrt(NCH))
    table = np.stack([cosine, sine], axis=0)[:, : NCH // 2]
    table = table.reshape(2, NCH // 2, KEEP // 2, 2).transpose(3, 0, 2, 1)
    return np.ascontiguousarray(table.reshape(2, KEEP, NCH // 2)).astype(ml_dtypes.bfloat16)


def spectra_kernel(
    rim, x_any, raw_ref, table_any, out_ref,
    x_ref, taps_ref, loose_ref, table_ref, fir_ref, wide_ref, acc_ref, x_sem, table_sem,
):
    blocks = 64 // INPUTS
    loads = [
        pltpu.make_async_copy(
            x_any.at[pl.ds(b * INPUTS, INPUTS)], x_ref.at[pl.ds(b * INPUTS, INPUTS)], x_sem.at[b]
        )
        for b in range(blocks)
    ]
    for load in loads:
        load.start()
    table_load = pltpu.make_async_copy(table_any, table_ref, table_sem)
    table_load.start()
    for cb in range(16):
        chunk = raw_ref[:, cb * LANES : (cb + 1) * LANES]
        for p in range(2):
            loose_ref[pl.ds(cb * 2 + p, TAPS, stride=33), :] = chunk
    for k in range(TAPS):
        taps_ref[k] = loose_ref[pl.ds(k * 33, 32), :]

    if rim:
        for rho in range(2 * GROUP):
            fir_ref[pl.ds(rho * PITCH, 64), :] = jnp.zeros((64, LANES), jnp.float32)

    def filter_input(i, carry):
        for piece in range(2):
            rows = slice(8 * piece, 8 * piece + 8)
            halves = []
            for part in range(2):
                taps = [taps_ref[k, pl.ds(16 * part + 8 * piece, 8), :] for k in range(TAPS)]
                frame = [
                    x_ref[i, t, pl.ds(16 * part, 16), :].astype(jnp.float32)[rows]
                    for t in range(TAPS)
                ]
                totals = []
                for t in range(1 if rim else 0, TAPS):
                    pairs = [(f, TAPS - t + f) for f in range(t)] if rim else [
                        (t + k, k) for k in range(TAPS - t)
                    ]
                    total = None
                    for f, k in pairs:
                        term = frame[f] * taps[k]
                        total = term if total is None else total + term
                    totals.append(total)
                halves.append(totals)
            for t, (early, late) in enumerate(zip(*halves), 1 if rim else 0):
                base = t * 64 + i + 8 * piece * PITCH
                fir_ref[pl.ds(base, 8, stride=PITCH), :] = early + late
                fir_ref[pl.ds(base + GROUP * PITCH, 8, stride=PITCH), :] = early - late
        return carry

    for b, load in enumerate(loads):
        load.wait()
        lax.fori_loop(b * INPUTS, (b + 1) * INPUTS, filter_input, 0, unroll=8)

    table_load.wait()
    def transform(low_bit, carry):
        for p in range(2):
            for cb in range(8):
                wide_ref[:, pl.ds(cb * LANES, LANES)] = fir_ref[
                    pl.ds((low_bit * GROUP + cb * 2 + p) * PITCH, 512), :
                ].astype(jnp.bfloat16)
            acc_ref[low_bit, p] = lax.dot_general(
                table_ref[low_bit],
                wide_ref[...],
                (((1,), (1,)), ((), ())),
                preferred_element_type=jnp.float32,
            )
        return carry

    lax.fori_loop(0, 2, transform, 0, unroll=True)

    low = lax.broadcasted_iota(jnp.int32, (128, LANES), 1) < 64
    for t2 in range(4):
        lanes = pl.ds(t2 * LANES, LANES)
        for p in range(2):
            pair = []
            for low_bit in range(2):
                cosine = acc_ref[low_bit, p, pl.ds(0, 128), lanes]
                sine = acc_ref[low_bit, 1 - p, pl.ds(128, 128), lanes]
                pair.append(cosine + sine if p == 0 else cosine - sine)
            zero, one = pair
            even = jnp.where(low, zero, pltpu.roll(one, 64, 1))
            odd = jnp.where(low, pltpu.roll(zero, 64, 1), one)
            row = p * 8 + 2 * t2
            fir_ref[pl.ds(row, 128, stride=17), :] = even
            fir_ref[pl.ds(row + 1, 128, stride=17), :] = odd
    for pair in range(128):
        out_ref[pl.ds(pair * 16, 16), :] = fir_ref[pl.ds(pair * 17, 16), :].astype(
            out_ref.dtype
        )


def spectra(x, taps, table, rim):
    return pl.pallas_call(
        functools.partial(spectra_kernel, rim),
        in_specs=[
            pl.BlockSpec(memory_space=pl.ANY),
            pl.BlockSpec(memory_space=pltpu.VMEM),
            pl.BlockSpec(memory_space=pl.ANY),
        ],
        out_specs=pl.BlockSpec(memory_space=pltpu.VMEM),
        out_shape=jax.ShapeDtypeStruct((2048, LANES), jnp.bfloat16 if rim else jnp.float32),
        scratch_shapes=[
            pltpu.VMEM((64, 8, 32, LANES), jnp.bfloat16),
            pltpu.VMEM((TAPS, 32, LANES), jnp.float32),
            pltpu.VMEM(((TAPS + 1) * 33, LANES), jnp.float32),
            pltpu.VMEM((2, KEEP, NCH // 2), jnp.bfloat16),
            pltpu.VMEM(((2 * GROUP + 1) * PITCH, LANES), jnp.float32),
            pltpu.VMEM((512, NCH // 2), jnp.bfloat16),
            pltpu.VMEM((2, 2, KEEP, 512), jnp.float32),
            pltpu.SemaphoreType.DMA((64 // INPUTS,)),
            pltpu.SemaphoreType.DMA,
        ],
        compiler_params=pltpu.CompilerParams(vmem_limit_bytes=(56 if rim else 24) * MIB),
        cost_estimate=pl.CostEstimate(
            flops=2 * 512 * 2048 * 512, bytes_accessed=6 * MIB, transcendentals=0
        ),
    )(x, taps, table)


def prepared(voltages, fir_taps):
    x = voltages.reshape(64, 8, 2, 16, LANES).transpose(0, 1, 3, 2, 4).reshape(64, 8, 32, LANES)
    return x, fir_taps


def correlate_kernel(late, place_ref, *refs):
    if late:
        left_ref, cols = refs[0], refs[1:5]
        out_ref, full_ref, sem = refs[-3:]
    else:
        rows, cols = refs[:4], list(refs[4:7])
        out_ref, left_ref, full_ref, sem, mine_ref, mine_sem = refs[-6:]
        load = pltpu.make_async_copy(cols[0], mine_ref, mine_sem)
        load.start()
        load.wait()
        cols[0] = mine_ref
    odd = place_ref[5] == 1
    half = 1 - place_ref[4] if late else place_ref[4]
    lane = pl.multiple_of(half * LANES, LANES)

    def store(step):
        return pltpu.make_async_copy(
            full_ref.at[step],
            out_ref.at[pl.ds(2 * step, 2), :, :, pl.ds(lane, LANES)],
            sem.at[step],
        )

    def pair_of_channels(step, carry):
        at = pl.ds(pl.multiple_of(step * 16, 16), 16)

        def block(ref):
            return ref[:, at, :].reshape(256, LANES)

        if late:
            tail = pl.ds(pl.multiple_of(step % 4 * 16, 16), 16)
            far = jnp.where(step < 4, cols[2][:, tail, :], cols[3][:, tail, :])
            far = far.reshape(256, LANES)
            right_blocks = [
                jnp.where(odd, block(cols[1]), far), jnp.where(odd, far, block(cols[0]))
            ]
        else:
            left_blocks = [block(ref) for ref in rows]
            mine = block(cols[0])
            right_blocks = [
                jnp.where(odd, block(cols[1]), mine), jnp.where(odd, mine, block(cols[2]))
            ]
        for channel in range(2):
            lanes = slice(64 * channel, 64 * channel + 64)
            if late:
                left = left_ref[2 * step + channel]
            else:
                left = jnp.concatenate([b[:, lanes] for b in left_blocks], axis=1).T
                left_ref[2 * step + channel] = left
            right = jnp.concatenate([b[:, lanes] for b in right_blocks], axis=1)
            pairs = right.astype(jnp.float32).reshape(16, 2, 8, LANES)
            flipped = jnp.concatenate([-pairs[:, 1:], pairs[:, :1]], axis=1)
            flipped = flipped.reshape(256, LANES).astype(jnp.bfloat16)
            product = lax.dot_general(
                left,
                jnp.concatenate([right, flipped], axis=1),
                (((1,), (0,)), ((), ())),
                preferred_element_type=jnp.float32,
            ) * (1.0 / 128.0)
            for k in range(4):
                where = pl.ds(pl.multiple_of(place_ref[k] * 64, 64), 64)
                for part in range(2):
                    full_ref[step, channel, part, where, :] = product[
                        k * 64 : (k + 1) * 64, part * LANES : (part + 1) * LANES
                    ]
        store(step).start()
        return carry

    lax.fori_loop(0, 8, pair_of_channels, 0, unroll=UNROLL)
    for step in range(8):
        store(step).wait()


def correlate(place, rows, cols, earlier):
    late = earlier is not None
    operands = [*rows, *cols]
    in_specs = [pl.BlockSpec(memory_space=pltpu.SMEM)]
    in_specs += [pl.BlockSpec(memory_space=pltpu.VMEM) for _ in operands]
    scratch = [
        pltpu.VMEM((8, 2, 2, 256, LANES), jnp.float32),
        pltpu.SemaphoreType.DMA((8,)),
    ]
    if not late:
        in_specs[5] = pl.BlockSpec(memory_space=pl.ANY)
        scratch += [pltpu.VMEM((16, 128, LANES), jnp.bfloat16), pltpu.SemaphoreType.DMA]
    aliases = {}
    out_specs = [pl.BlockSpec(memory_space=pl.ANY)]
    out_shape = [jax.ShapeDtypeStruct((16, 2, 256, 256), jnp.float32)]
    if not late:
        out_specs.append(pl.BlockSpec(memory_space=pltpu.VMEM))
        out_shape.append(jax.ShapeDtypeStruct((16, 256, 256), jnp.bfloat16))
    if late:
        in_specs.append(pl.BlockSpec(memory_space=pl.ANY))
        aliases = {1 + len(operands): 0}
        operands.append(earlier)
    return pl.pallas_call(
        functools.partial(correlate_kernel, late),
        in_specs=in_specs,
        out_specs=out_specs,
        out_shape=out_shape,
        scratch_shapes=scratch,
        input_output_aliases=aliases,
        compiler_params=pltpu.CompilerParams(vmem_limit_bytes=20 * MIB),
        cost_estimate=pl.CostEstimate(
            flops=2**29, bytes_accessed=8 * MIB, transcendentals=0
        ),
    )(place, *operands)


def per_device(voltages, fir_taps, table):
    x, taps = prepared(voltages, fir_taps)
    pre = spectra(x, taps, table, True)
    own = spectra(x, taps, table, False)
    own = own.reshape(16, 128, LANES)
    pre = pre.reshape(16, 128, LANES)
    row, col = lax.axis_index("row"), lax.axis_index("col")
    place = jnp.stack([col, col ^ 1, col ^ 2, col ^ 3, row // 2, row % 2]).astype(jnp.int32)
    ring = range(4)
    up = [(r, (r + 1) % 4) for r in ring]
    down = [(r, (r - 1) % 4) for r in ring]
    rim = lax.ppermute(pre, "chan", [(s, s - 1) for s in range(1, 16)])
    whole = (own + rim.astype(jnp.float32)).astype(jnp.bfloat16)
    turned = lax.all_to_all(whole, "chan", split_axis=0, concat_axis=0, tiled=True)
    crossed = lax.ppermute(
        turned, ("row", "col"), [(4 * r + c, 4 * c + r) for r in ring for c in ring]
    )
    far = lax.ppermute(turned, "col", [(c, c ^ 2) for c in ring])
    near = lax.ppermute(turned, "col", [(c, c ^ 1) for c in ring])
    both = lax.ppermute(far, "col", [(c, c ^ 1) for c in ring])
    lower = lax.ppermute(crossed, "row", up)
    upper = lax.ppermute(crossed, "row", down)
    tails = [lax.ppermute(lower[:, :64], "row", up), lax.ppermute(upper[:, 64:], "row", down)]
    rows = [turned, near, far, both]
    result, left = correlate(place, rows, [crossed, lower, upper], None)
    return correlate(place, [left], [lower, upper, *tails], result)[0]


def solution(mesh):
    table = dft_table()

    def run(voltages, fir_taps):
        return jax.shard_map(
            per_device,
            mesh=mesh,
            in_specs=(P(("row", "col"), "chan", None, None), P(), P()),
            out_specs=P("chan", None, "row", "col"),
            check_vma=False,
        )(voltages, fir_taps, jnp.asarray(table))

    return run
```
